1024 devices in a mesh: blk: 64 (over z, y), rep: 16 (over x, core).
Axes of the slice: x: 8, y: 8, z: 8, core: 2. Of those that a mesh axis runs over, the one named last changes fastest.
Arguments:
- features: bfloat16 [32768, 256], P('blk'), may hold values from -6 to 6
- weight: bfloat16 [256, 256], replicated, may hold values from -0.375 to 0.375
- cotangent: bfloat16 [32768, 256], P(('blk', 'rep')), may hold values from -6 to 6
- tile_values: bfloat16 [64, 64, 12, 128, 128], P('blk', 'rep'), may hold values from -0.0546875 to 0.0546875
- tile_rows: int32 [64, 64, 12], P('blk', 'rep'), may hold values from 0 to 3, as said below
- tile_cols: int32 [64, 64, 12], P('blk', 'rep'), may hold values from 0 to 3
- tile_count: int32 [64, 64], P('blk', 'rep'), may hold values from 1 to 12, as said below
Outputs:
- activations: bfloat16 [32768, 256], P(('blk', 'rep'))
- weight_grad: float32 [256, 256], replicated
- feature_grad: bfloat16 [32768, 256], P(('blk', 'rep'))
The draws below stay inside these ranges and needn't reach their ends.
Inputs may be any that keep to these rules, and one draw needn't show every extreme that they name: Among the live slots of one list the pairs (tile_rows, tile_cols) are distinct. `tile_count`: the list of a block with itself (offset 0) always has 12 live slots.
All inputs are finite; a program needn't handle non-finite values.
Results may differ from the reference program's by a relative error of at most 0.024.
Values may be sent and summed in bfloat16 or wider, within the bound.
No kernel may reach another device: no remote copies, remote signals or barrier semaphores. Data moves between devices by JAX's collectives and lax.ppermute only.
A program may use at most 32 MiB of HBM per device.

```python
import math
import jax
import jax.numpy as jnp
from jax import lax

WIDTH = 256
ROWS = 512
SLOTS = 12
BLOCKS = 64
NODES = 32768


def tile_layout(key):
    row_tiles = ROWS // 128
    positions = row_tiles * row_tiles
    scores = jax.random.randint(key, (BLOCKS, BLOCKS, positions), 0, 1 << 20) * positions
    scores = scores + jnp.arange(positions, dtype=jnp.int32)
    order = jnp.argsort(scores, axis=-1)[..., :SLOTS].astype(jnp.int32)
    heavy = jax.random.randint(jax.random.fold_in(key, 1), (BLOCKS, 1), 0, SLOTS // 2 + 1)
    extra = jax.random.randint(jax.random.fold_in(key, 2), (BLOCKS, BLOCKS), 1, SLOTS // 2 + 1)
    count = jnp.clip(heavy + extra, 1, SLOTS).astype(jnp.int32)
    count = count.at[:, 0].set(SLOTS)
    return (order // row_tiles, order % row_tiles, count)


def draw_tile_rows(key, part):
    rows, cols, count = tile_layout(key)
    return rows.astype(jnp.int32)


def draw_tile_cols(key, part):
    rows, cols, count = tile_layout(key)
    return cols.astype(jnp.int32)


def draw_tile_count(key, part):
    rows, cols, count = tile_layout(key)
    return count.astype(jnp.int32)


def block_levels(stream_key, extent, pieces, least, high):
    def one(dim, shards_of):
        steps = jax.random.uniform(jax.random.fold_in(jax.random.fold_in(stream_key, 6), dim), (shards_of,), jnp.float32, least / len(pieces), high / len(pieces))
        return jnp.repeat(jnp.exp(steps), extent[dim] // shards_of).reshape((-1,) + (1,) * (len(extent) - dim - 1))

    gain = one(*pieces[0])
    for cut in pieces[1:]:
        gain = gain * one(*cut)
    return gain


def scatter_about(own_key, extent, width, limit, split=(), kind=jnp.bfloat16):
    entries = width * jax.random.normal(own_key, extent, jnp.float32)
    if split:
        entries = entries * block_levels(own_key, extent, split, -0.22, 0.18)
    return jnp.clip(entries, -limit, limit).astype(kind)


def setup_inputs(seed: int = 0) -> dict:
    key_list = jax.random.split(jax.random.key(seed), 8)
    return {
        "features": scatter_about(key_list[0], (NODES, WIDTH), 1.0, 6.0, ((0, 64),)),
        "weight": scatter_about(key_list[1], (WIDTH, WIDTH), WIDTH ** -0.5, 0.375),
        "cotangent": scatter_about(key_list[2], (NODES, WIDTH), 1.0, 6.0, ((0, 1024),)),
        "tile_values": scatter_about(key_list[3], (BLOCKS, BLOCKS, SLOTS, 128, 128), (BLOCKS * SLOTS * 8192 // ROWS) ** -0.5, 0.0546875, ((0, 64), (1, 16))),
        "tile_rows": draw_tile_rows(jax.random.fold_in(key_list[7], 71), 0),
        "tile_cols": draw_tile_cols(jax.random.fold_in(key_list[7], 71), 0),
        "tile_count": draw_tile_count(jax.random.fold_in(key_list[7], 71), 0),
    }


def aggregate(tile_values, tile_rows, tile_cols, tile_count, features):
    row_tiles = ROWS // 128
    blocks = features.reshape(BLOCKS, row_tiles, 128, WIDTH)
    slot_ids = jnp.arange(SLOTS, dtype=jnp.int32)
    offsets = jnp.arange(BLOCKS, dtype=jnp.int32)

    def one_block(index):
        rolled = jnp.roll(blocks, -index, axis=0)
        tiles = lax.dynamic_index_in_dim(tile_values, index, 0, False).astype(jnp.float32)
        rows = lax.dynamic_index_in_dim(tile_rows, index, 0, False)
        cols = lax.dynamic_index_in_dim(tile_cols, index, 0, False)
        count = lax.dynamic_index_in_dim(tile_count, index, 0, False)
        live = (slot_ids[None, :] < count[:, None]).astype(jnp.float32)
        picked = rolled[offsets[:, None], cols].astype(jnp.float32)
        product = jnp.einsum('osij,osjf->osif', tiles, picked, precision=lax.Precision.HIGHEST)
        product = product * live[:, :, None, None]
        row_hot = (rows[:, :, None] == jnp.arange(row_tiles, dtype=jnp.int32)).astype(jnp.float32)
        return jnp.einsum('osr,osif->rif', row_hot, product, precision=lax.Precision.HIGHEST)
    return lax.map(one_block, offsets).reshape(NODES, WIDTH)

def spread_back(tile_values, tile_rows, tile_cols, tile_count, grads):
    row_tiles = ROWS // 128
    blocks = grads.reshape(BLOCKS, row_tiles, 128, WIDTH)
    slot_ids = jnp.arange(SLOTS, dtype=jnp.int32)

    def step(total, index):
        tiles = lax.dynamic_index_in_dim(tile_values, index, 0, False).astype(jnp.float32)
        rows = lax.dynamic_index_in_dim(tile_rows, index, 0, False)
        cols = lax.dynamic_index_in_dim(tile_cols, index, 0, False)
        count = lax.dynamic_index_in_dim(tile_count, index, 0, False)
        live = (slot_ids[None, :] < count[:, None]).astype(jnp.float32)
        mine = lax.dynamic_index_in_dim(blocks, index, 0, False)
        picked = mine[rows].astype(jnp.float32)
        product = jnp.einsum('osij,osif->osjf', tiles, picked, precision=lax.Precision.HIGHEST)
        product = product * live[:, :, None, None]
        col_hot = (cols[:, :, None] == jnp.arange(row_tiles, dtype=jnp.int32)).astype(jnp.float32)
        contrib = jnp.einsum('osc,osjf->ocjf', col_hot, product, precision=lax.Precision.HIGHEST)
        return (total + jnp.roll(contrib, index, axis=0), None)
    start = jnp.zeros((BLOCKS, row_tiles, 128, WIDTH), jnp.float32)
    total, unused = lax.scan(step, start, jnp.arange(BLOCKS, dtype=jnp.int32))
    return total.reshape(NODES, WIDTH)

def reference(features, weight, cotangent, tile_values, tile_rows, tile_cols, tile_count):
    agg = aggregate(tile_values, tile_rows, tile_cols, tile_count, features).astype(jnp.bfloat16)
    z_value = jnp.dot(agg, weight, preferred_element_type=jnp.float32)
    sigma = jax.nn.sigmoid(z_value)
    activations = (z_value * sigma).astype(jnp.bfloat16)
    dz_value = (cotangent.astype(jnp.float32) * sigma * (1.0 + z_value * (1.0 - sigma))).astype(jnp.bfloat16)
    weight_grad = jnp.dot(agg.T, dz_value, preferred_element_type=jnp.float32) / math.sqrt(NODES)
    dy_value = jnp.dot(dz_value, weight.T, preferred_element_type=jnp.float32).astype(jnp.bfloat16)
    feature_grad = spread_back(tile_values, tile_rows, tile_cols, tile_count, dy_value).astype(jnp.bfloat16)
    return (activations, weight_grad, feature_grad)
```

```python
import math

import jax
import jax.numpy as jnp
from jax import lax
from jax.experimental import pallas as pl
from jax.experimental.pallas import tpu as pltpu
from jax.sharding import Mesh
from jax.sharding import PartitionSpec as P

TILE = 128
BF16 = jnp.bfloat16
F32 = jnp.float32
VMEM = pl.BlockSpec(memory_space=pltpu.VMEM)
SMEM = pl.BlockSpec(memory_space=pltpu.SMEM)
ANY = pl.BlockSpec(memory_space=pl.ANY)


def params(mib=40):
    return pltpu.CompilerParams(vmem_limit_bytes=mib << 20)


def shape_of(shape, dtype=BF16):
    return jax.ShapeDtypeStruct(shape, dtype)


def cost(flops, nbytes):
    return pl.CostEstimate(flops=flops, bytes_accessed=nbytes, transcendentals=0)


def dense_kernel(rows, cols, count, tiles, out):
    section = pl.program_id(0)
    out[...] = jnp.zeros_like(out)
    for slot in range(tiles.shape[1]):

        @pl.when(slot < count[section])
        def _():
            row = pl.multiple_of(rows[section, slot] * TILE, TILE)
            col = pl.multiple_of(cols[section, slot] * TILE, TILE)
            out[0, pl.ds(row, TILE), pl.ds(col, TILE)] = tiles[0, slot]


def dense_blocks(tiles, rows, cols, count, rows_blk):
    sections, slots = tiles.shape[:2]
    return pl.pallas_call(
        dense_kernel,
        grid=(sections,),
        out_shape=shape_of((sections, rows_blk, rows_blk)),
        in_specs=[
            SMEM,
            SMEM,
            SMEM,
            pl.BlockSpec((1, slots, TILE, TILE), lambda i: (i, 0, 0, 0)),
        ],
        out_specs=pl.BlockSpec((1, rows_blk, rows_blk), lambda i: (i, 0, 0)),
        compiler_params=params(),
        cost_estimate=cost(0, tiles.size * 2 + sections * rows_blk * rows_blk * 2),
        name="dense_blocks",
    )(rows, cols, count, tiles)


def window_kernel(pos, planes, out, sems):
    depth, sections = planes.shape[0], out.shape[0]
    first = pos[0] + pos[2]
    copies = []
    for target in range(sections):
        plane = lax.rem(first + (target > pos[1]).astype(jnp.int32), depth)
        copies.append(pltpu.make_async_copy(planes.at[plane], out.at[target], sems.at[target]))
    for copy in copies:
        copy.start()
    for copy in copies:
        copy.wait()


def window_pieces(pos, planes, sections):
    shape = (sections,) + planes.shape[1:]
    return pl.pallas_call(
        window_kernel,
        out_shape=shape_of(shape),
        in_specs=[SMEM, ANY],
        out_specs=ANY,
        scratch_shapes=[pltpu.SemaphoreType.DMA((sections,))],
        compiler_params=params(),
        cost_estimate=cost(0, math.prod(shape) * 4),
        name="window_pieces",
    )(pos, planes)


def block_order(pos, sections, own, section):
    core = pos[3] if own else 1 - pos[3]
    return lax.rem(pos[1] + core * (sections // 2) + section, sections)


def forward_kernel(pos, mine, other, mine_block, other_block, cot, out, total):
    section = pl.program_id(0)
    rows = total.shape[0]
    here = jnp.dot(mine[0], mine_block[0], preferred_element_type=F32) + jnp.dot(
        other[0], other_block[0], preferred_element_type=F32
    )

    @pl.when(section == 0)
    def _():
        total[...] = here

    @pl.when(section > 0)
    def _():
        total[...] += here

    @pl.when(section == pl.num_programs(0) - 1)
    def _():
        half, width = cot.shape[0], out.shape[1]
        out[:rows, :] = total[...].astype(BF16)
        out[rows : rows + half, :] = cot[:, :width]
        out[rows + half :, :] = cot[:, width:]


def forward_part(pos, mine, other, blocks, cot):
    half, rows = mine.shape[:2]
    sections, _, width = blocks.shape
    extra = 2 * cot.shape[0]

    def block_spec(own):
        return pl.BlockSpec(
            (1, rows, width), lambda i, pos: (block_order(pos, sections, own, i), 0, 0)
        )

    matrix = pl.BlockSpec((1, rows, rows), lambda i, pos: (i, 0, 0))
    return pl.pallas_call(
        forward_kernel,
        out_shape=shape_of((rows + extra, width)),
        grid_spec=pltpu.PrefetchScalarGridSpec(
            num_scalar_prefetch=1,
            grid=(half,),
            in_specs=[
                matrix,
                matrix,
                block_spec(True),
                block_spec(False),
                pl.BlockSpec(cot.shape, lambda i, pos: (0, 0)),
            ],
            out_specs=pl.BlockSpec((rows + extra, width), lambda i, pos: (0, 0)),
            scratch_shapes=[pltpu.VMEM((rows, width), F32)],
        ),
        compiler_params=params(),
        cost_estimate=cost(
            2 * sections * rows * rows * width, sections * rows * (rows + width) * 2
        ),
        name="forward_part",
    )(pos, mine, other, blocks, blocks, cot)


def aggregate_kernel(parts, out):
    rows = out.shape[0] // 2
    ranks = parts.shape[0]
    extra = rows // ranks
    total = parts[0, :rows, :].astype(F32)
    for rank in range(1, ranks):
        total += parts[rank, :rows, :].astype(F32)
    out[:rows, :] = total.astype(BF16)
    for rank in range(ranks):
        out[rows + rank * extra : rows + (rank + 1) * extra, :] = parts[rank, rows:, :]


def aggregate_part(parts, rows):
    shape = (2 * rows, parts.shape[2])
    return pl.pallas_call(
        aggregate_kernel,
        out_shape=shape_of(shape),
        in_specs=[VMEM],
        out_specs=VMEM,
        compiler_params=params(),
        cost_estimate=cost(parts.size, parts.size * 2 + math.prod(shape) * 2),
        name="aggregate_part",
    )(parts)


def layer_kernel(ranks, pos, pair, weight, mine, other, act, out, act_all, dz_all, term):
    rows = pair.shape[1] // 2
    width = pair.shape[2]
    own = act.shape[0]
    both = 2 * own
    for rank in range(ranks):
        span = slice(rank * both, (rank + 1) * both)
        z_value = jnp.dot(pair[0, span, :], weight[:width, :], preferred_element_type=F32)
        z_value += jnp.dot(pair[1, span, :], weight[width:, :], preferred_element_type=F32)
        start = rows + rank * both
        cot = jnp.concatenate(
            [
                jnp.concatenate(
                    [pair[core, start + side * own : start + (side + 1) * own, :] for side in (0, 1)],
                    axis=1,
                )
                for core in (0, 1)
            ],
            axis=0,
        ).astype(F32)
        sigma = jax.nn.sigmoid(z_value)
        act_all[span, :] = (z_value * sigma).astype(BF16)
        dz_all[span, :] = (cot * sigma * (1.0 + z_value * (1.0 - sigma))).astype(BF16)
    x_index, core = pos[2], pos[3]
    act[...] = act_all[pl.ds(pl.multiple_of((2 * x_index + core) * own, own), own), :]
    dz_value = dz_all[...]
    contract_rows = (((0,), (0,)), ((), ()))
    contract_cols = (((1,), (1,)), ((), ()))
    term[...] = lax.dot_general(
        pair[core, :rows, :], dz_value, contract_rows, preferred_element_type=F32
    )
    weight_rows = weight[pl.ds(pl.multiple_of(core * width, width), width), :]
    dy_turned = lax.dot_general(
        weight_rows, dz_value, contract_cols, preferred_element_type=F32
    ).astype(BF16)
    chunk = width // ranks
    piece = term[pl.ds(pl.multiple_of(x_index * chunk, chunk), chunk), :].astype(BF16)
    piece = jnp.concatenate([piece[:, :width], piece[:, width:]], axis=0)
    sections = out.shape[0]
    for is_own, matrices in ((True, mine), (False, other)):
        for section in range(sections // 2):
            grads = jnp.dot(dy_turned, matrices[section], preferred_element_type=F32)
            target = block_order(pos, sections, is_own, section)
            out[target, :rows, :] = grads.astype(BF16).T
    for target in range(sections):
        out[target, rows:, :] = piece


def layer_part(pos, pair, weight, mine, other, ranks):
    rows, width = pair.shape[1] // 2, pair.shape[2]
    sections = 2 * mine.shape[0]
    own = rows // (2 * ranks)
    out = (sections, rows + 2 * width // ranks, width)

    def kernel(*refs):
        layer_kernel(ranks, *refs)

    return pl.pallas_call(
        kernel,
        out_shape=(shape_of((own, 2 * width)), shape_of(out)),
        in_specs=[SMEM] + [VMEM] * 4,
        out_specs=(VMEM, VMEM),
        scratch_shapes=[
            pltpu.VMEM((rows, 2 * width), BF16),
            pltpu.VMEM((rows, 2 * width), BF16),
            pltpu.VMEM((width, 2 * width), F32),
        ],
        compiler_params=params(),
        cost_estimate=cost(
            2 * sections * rows * rows * width, mine.size * 4 + math.prod(out) * 2
        ),
        name="layer_part",
    )(pos, pair, weight, mine, other)


def planes_kernel(rows, pos, parts, out):
    sections = parts.shape[0]
    ranks = out.shape[0]
    share = rows // ranks
    for rank in range(ranks):
        span = slice(rank * share, (rank + 1) * share)
        near = jnp.zeros((share, parts.shape[2]), F32)
        far = near
        for source in range(sections):
            value = parts[source, span, :].astype(F32)
            same = source <= pos[1]
            near += jnp.where(same, value, 0.0)
            far += jnp.where(same, 0.0, value)
        out[rank, :share, :] = near.astype(BF16)
        out[rank, share : 2 * share, :] = far.astype(BF16)
    term = parts[0, rows:, :].astype(F32)
    for source in range(1, sections):
        term += parts[source, rows:, :].astype(F32)
    for rank in range(ranks):
        out[rank, 2 * share :, :] = term.astype(BF16)


def planes_part(pos, parts, rows, ranks):
    extra = parts.shape[1] - rows
    shape = (ranks, 2 * rows // ranks + extra, parts.shape[2])

    def kernel(*refs):
        planes_kernel(rows, *refs)

    return pl.pallas_call(
        kernel,
        out_shape=shape_of(shape),
        in_specs=[SMEM, VMEM],
        out_specs=VMEM,
        compiler_params=params(),
        cost_estimate=cost(parts.size * 2, parts.size * 2 + math.prod(shape) * 2),
        name="planes_part",
    )(pos, parts)


def depth_kernel(share, pos, parts, out):
    ranks = parts.shape[0]
    depth = out.shape[0]
    extra = parts.shape[1] - 2 * share
    for target in range(depth):
        near = lax.rem(target - pos[0] + depth, depth)
        far = lax.rem(target - pos[0] + 2 * depth - 1, depth)
        value = parts[near, :share, :].astype(F32) + parts[far, share : 2 * share, :].astype(F32)
        out[target, :share, :] = value.astype(BF16)
        for rank in range(ranks):
            out[target, share + rank * extra : share + (rank + 1) * extra, :] = parts[
                rank, 2 * share :, :
            ]


def depth_part(pos, parts, share, depth):
    ranks, height, width = parts.shape
    shape = (depth, share + ranks * (height - 2 * share), width)

    def kernel(*refs):
        depth_kernel(share, *refs)

    return pl.pallas_call(
        kernel,
        out_shape=shape_of(shape),
        in_specs=[SMEM, VMEM],
        out_specs=VMEM,
        compiler_params=params(),
        cost_estimate=cost(parts.size, parts.size * 2 + math.prod(shape) * 2),
        name="depth_part",
    )(pos, parts)


def total_kernel(parts, out):
    total = parts[0].astype(F32)
    for source in range(1, parts.shape[0]):
        total += parts[source].astype(F32)
    out[...] = total.astype(BF16)


def total_part(parts):
    return pl.pallas_call(
        total_kernel,
        out_shape=shape_of(parts.shape[1:]),
        in_specs=[VMEM],
        out_specs=VMEM,
        compiler_params=params(),
        cost_estimate=cost(parts.size, parts.size * 2),
        name="total_part",
    )(parts)


def finish_kernel(ranks, scale, pos, pair, term, grads):
    width = pair.shape[2]
    own = grads.shape[0]
    start = pl.multiple_of(pos[3] * own, own)
    for core in (0, 1):
        side = slice(core * width, (core + 1) * width)
        grads[:, side] = pair[core, pl.ds(start, own), :]
    chunk = width // ranks
    for core in (0, 1):
        for rank in range(ranks):
            row = core * width + rank * chunk
            for side in (0, 1):
                first = 2 * own + (2 * rank + side) * chunk
                value = pair[core, first : first + chunk, :].astype(F32) / scale
                term[row : row + chunk, side * width : (side + 1) * width] = value


def finish_part(pos, pair, ranks, own, nodes):
    width = pair.shape[2]

    def kernel(*refs):
        finish_kernel(ranks, math.sqrt(nodes), *refs)

    return pl.pallas_call(
        kernel,
        out_shape=(shape_of((2 * width, 2 * width), F32), shape_of((own, 2 * width))),
        in_specs=[SMEM, VMEM],
        out_specs=(VMEM, VMEM),
        compiler_params=params(),
        cost_estimate=cost(0, pair.size * 2),
        name="finish_part",
    )(pos, pair)


def exchange(pieces, axis):
    return lax.all_to_all(pieces, axis, split_axis=0, concat_axis=0, tiled=True)


def per_device(features, weight, cotangent, tile_values, tile_rows, tile_cols, tile_count):
    rows, columns = features.shape
    width = columns // 2
    depth, sections, ranks = lax.axis_size("z"), lax.axis_size("y"), lax.axis_size("x")
    nodes = rows * depth * sections
    own = rows // (2 * ranks)
    core = lax.axis_index("core")
    pos = jnp.stack(
        [lax.axis_index("z"), lax.axis_index("y"), lax.axis_index("x"), core]
    ).astype(jnp.int32)

    mine = dense_blocks(tile_values[0], tile_rows[0], tile_cols[0], tile_count[0], rows)
    other = lax.ppermute(mine, "core", [(0, 1), (1, 0)])

    half = lax.dynamic_slice_in_dim(features, core * width, width, axis=1)
    planes = lax.all_gather(half, "z", axis=0, tiled=False)
    blocks = exchange(window_pieces(pos, planes, sections), "y")
    part = forward_part(pos, mine, other, blocks, cotangent)
    parts = lax.all_gather(part, "x", axis=0, tiled=False)
    pair = lax.all_gather(aggregate_part(parts, rows), "core", axis=0, tiled=False)
    activations, pieces = layer_part(pos, pair, weight, mine, other, ranks)
    pieces = exchange(pieces, "y")
    pieces = exchange(planes_part(pos, pieces, rows, ranks), "x")
    pieces = exchange(depth_part(pos, pieces, rows // ranks, depth), "z")
    pair = lax.all_gather(total_part(pieces), "core", axis=0, tiled=False)
    weight_grad, feature_grad = finish_part(pos, pair, ranks, own, nodes)
    return (activations, weight_grad, feature_grad)


def solution(mesh):
    blk, rep = mesh.devices.shape
    ranks = rep // 2
    devices = mesh.devices.reshape(ranks, blk // ranks, ranks, 2)
    grid = Mesh(devices, ("z", "y", "x", "core"))
    blk_axes, rep_axes = ("z", "y"), ("x", "core")
    return jax.shard_map(
        per_device,
        mesh=grid,
        in_specs=(
            P(blk_axes, None),
            P(),
            P(blk_axes + rep_axes, None),
            P(blk_axes, rep_axes, None, None, None),
            P(blk_axes, rep_axes, None),
            P(blk_axes, rep_axes, None),
            P(blk_axes, rep_axes),
        ),
        out_specs=(P(blk_axes + rep_axes, None), P(), P(blk_axes + rep_axes, None)),
        check_vma=False,
    )
```

```python
import math

import jax
import jax.numpy as jnp
from jax import lax
from jax.experimental import pallas as pl
from jax.experimental.pallas import tpu as pltpu
from jax.sharding import Mesh
from jax.sharding import PartitionSpec as P

TILE = 128
BF16 = jnp.bfloat16
F32 = jnp.float32
VMEM = pl.BlockSpec(memory_space=pltpu.VMEM)
SMEM = pl.BlockSpec(memory_space=pltpu.SMEM)
ANY = pl.BlockSpec(memory_space=pl.ANY)


def params(mib=40):
    return pltpu.CompilerParams(vmem_limit_bytes=mib << 20)


def shape_of(shape, dtype=BF16):
    return jax.ShapeDtypeStruct(shape, dtype)


def cost(flops, nbytes):
    return pl.CostEstimate(flops=flops, bytes_accessed=nbytes, transcendentals=0)


def dense_kernel(rows, cols, count, tiles, out):
    section = pl.program_id(0)
    out[...] = jnp.zeros_like(out)
    for slot in range(tiles.shape[1]):

        @pl.when(slot < count[section])
        def _():
            row = pl.multiple_of(rows[section, slot] * TILE, TILE)
            col = pl.multiple_of(cols[section, slot] * TILE, TILE)
            out[0, pl.ds(row, TILE), pl.ds(col, TILE)] = tiles[0, slot]


def dense_blocks(tiles, rows, cols, count, rows_blk):
    sections, slots = tiles.shape[:2]
    return pl.pallas_call(
        dense_kernel,
        grid=(sections,),
        out_shape=shape_of((sections, rows_blk, rows_blk)),
        in_specs=[
            SMEM,
            SMEM,
            SMEM,
            pl.BlockSpec((1, slots, TILE, TILE), lambda i: (i, 0, 0, 0)),
        ],
        out_specs=pl.BlockSpec((1, rows_blk, rows_blk), lambda i: (i, 0, 0)),
        compiler_params=params(),
        cost_estimate=cost(0, tiles.size * 2 + sections * rows_blk * rows_blk * 2),
        name="dense_blocks",
    )(rows, cols, count, tiles)


def window_kernel(pos, planes, out):
    depth = planes.shape[0]
    ranks = depth
    for target in range(out.shape[0]):
        ahead = (target // ranks > pos[1]).astype(jnp.int32)
        plane = lax.rem(pos[0] + target % ranks + ahead, depth)
        out[target] = planes[plane]


def window_pieces(pos, planes, sections, ranks):
    shape = (sections * ranks,) + planes.shape[1:]
    return pl.pallas_call(
        window_kernel,
        out_shape=shape_of(shape),
        in_specs=[SMEM, VMEM],
        out_specs=VMEM,
        compiler_params=params(),
        cost_estimate=cost(0, math.prod(shape) * 2),
        name="window_pieces",
    )(pos, planes)


def block_order(pos, sections, own, section):
    core = pos[3] if own else 1 - pos[3]
    return lax.rem(pos[1] + core * (sections // 2) + section, sections)


def fetch(other, held, sem):
    return pltpu.make_async_copy(other, held, sem)


def forward_kernel(pos, mine, other, blocks, out, held, sem):
    copy = fetch(other, held, sem)
    copy.start()
    half = mine.shape[0]
    sections = blocks.shape[0]
    total = jnp.zeros(out.shape, F32)
    for is_own, matrices in ((True, mine), (False, held)):
        if not is_own:
            copy.wait()
        for section in range(half):
            block = blocks[block_order(pos, sections, is_own, section)]
            total += jnp.dot(matrices[section], block, preferred_element_type=F32)
    out[...] = total.astype(BF16)


def forward_part(pos, mine, other, blocks):
    rows = mine.shape[1]
    sections, _, width = blocks.shape
    return pl.pallas_call(
        forward_kernel,
        out_shape=shape_of((rows, width)),
        in_specs=[SMEM, VMEM, ANY, VMEM],
        out_specs=VMEM,
        scratch_shapes=[pltpu.VMEM(other.shape, BF16), pltpu.SemaphoreType.DMA],
        compiler_params=params(),
        cost_estimate=cost(
            2 * sections * rows * rows * width, sections * rows * (rows + width) * 2
        ),
        name="forward_part",
    )(pos, mine, other, blocks)


def layer_kernel(parts, cot, weight, act, out):
    replicas, own, width = parts.shape
    ranks = replicas // 2
    sides = []
    for core in (0, 1):
        side = parts[core].astype(F32)
        for rank in range(1, ranks):
            side += parts[2 * rank + core].astype(F32)
        sides.append(side)
    agg = jnp.concatenate(sides, axis=1).astype(BF16)
    z_value = jnp.dot(agg, weight[...], preferred_element_type=F32)
    sigma = jax.nn.sigmoid(z_value)
    act[...] = (z_value * sigma).astype(BF16)
    slope = cot[...].astype(F32) * sigma * (1.0 + z_value * (1.0 - sigma))
    dz_value = slope.astype(BF16)
    dy_value = lax.dot_general(
        dz_value, weight[...], (((1,), (1,)), ((), ())), preferred_element_type=F32
    ).astype(BF16)
    term = lax.dot_general(
        agg, dz_value, (((0,), (0,)), ((), ())), preferred_element_type=F32
    ).astype(BF16)
    chunk = width // ranks
    for rank in range(ranks):
        for core in (0, 1):
            target = 2 * rank + core
            row = core * width + rank * chunk
            out[target, :own, :] = dy_value[:, core * width : (core + 1) * width]
            out[target, own : own + chunk, :] = term[row : row + chunk, :width]
            out[target, own + chunk :, :] = term[row : row + chunk, width:]


def layer_part(parts, cot, weight):
    replicas, own, width = parts.shape
    out = (replicas, own + 4 * width // replicas, width)
    return pl.pallas_call(
        layer_kernel,
        out_shape=(shape_of(cot.shape), shape_of(out)),
        in_specs=[VMEM] * 3,
        out_specs=(VMEM, VMEM),
        compiler_params=params(),
        cost_estimate=cost(6 * own * 4 * width * width, math.prod(out) * 4),
        name="layer_part",
    )(parts, cot, weight)


def backward_kernel(own, pos, parts, mine, other, out, held, sem):
    copy = fetch(other, held, sem)
    copy.start()
    replicas, _, width = parts.shape
    rows = replicas * own
    piece = parts[0, own:, :].astype(F32)
    for source in range(1, replicas):
        piece += parts[source, own:, :].astype(F32)
    piece = piece.astype(BF16)
    sections = out.shape[0]
    for target in range(sections):
        out[target, rows:, :] = piece
    dy_turned = parts[:, :own, :].reshape(rows, width).T
    for is_own, matrices in ((True, mine), (False, held)):
        if not is_own:
            copy.wait()
        for section in range(sections // 2):
            grads = jnp.dot(dy_turned, matrices[section], preferred_element_type=F32)
            target = block_order(pos, sections, is_own, section)
            out[target, :rows, :] = grads.astype(BF16).T


def backward_part(pos, parts, mine, other, own):
    replicas, height, width = parts.shape
    rows = replicas * own
    sections = 2 * mine.shape[0]
    out = (sections, rows + height - own, width)

    def kernel(*refs):
        backward_kernel(own, *refs)

    return pl.pallas_call(
        kernel,
        out_shape=shape_of(out),
        in_specs=[SMEM, VMEM, VMEM, ANY],
        out_specs=VMEM,
        scratch_shapes=[pltpu.VMEM(other.shape, BF16), pltpu.SemaphoreType.DMA],
        compiler_params=params(),
        cost_estimate=cost(
            2 * sections * rows * rows * width, mine.size * 4 + math.prod(out) * 2
        ),
        name="backward_part",
    )(pos, parts, mine, other)


def planes_kernel(rows, pos, parts, out):
    sections = parts.shape[0]
    ranks = out.shape[0]
    share = rows // ranks
    for rank in range(ranks):
        span = slice(rank * share, (rank + 1) * share)
        near = jnp.zeros((share, parts.shape[2]), F32)
        far = near
        for source in range(sections):
            value = parts[source, span, :].astype(F32)
            same = source <= pos[1]
            near += jnp.where(same, value, 0.0)
            far += jnp.where(same, 0.0, value)
        out[rank, :share, :] = near.astype(BF16)
        out[rank, share : 2 * share, :] = far.astype(BF16)
    term = parts[0, rows:, :].astype(F32)
    for source in range(1, sections):
        term += parts[source, rows:, :].astype(F32)
    for rank in range(ranks):
        out[rank, 2 * share :, :] = term.astype(BF16)


def planes_part(pos, parts, rows, ranks):
    extra = parts.shape[1] - rows
    shape = (ranks, 2 * rows // ranks + extra, parts.shape[2])

    def kernel(*refs):
        planes_kernel(rows, *refs)

    return pl.pallas_call(
        kernel,
        out_shape=shape_of(shape),
        in_specs=[SMEM, VMEM],
        out_specs=VMEM,
        compiler_params=params(),
        cost_estimate=cost(parts.size * 2, parts.size * 2 + math.prod(shape) * 2),
        name="planes_part",
    )(pos, parts)


def depth_kernel(share, pos, parts, out):
    ranks = parts.shape[0]
    depth = out.shape[0]
    extra = parts.shape[1] - 2 * share
    for target in range(depth):
        near = lax.rem(target - pos[0] + depth, depth)
        far = lax.rem(target - pos[0] + 2 * depth - 1, depth)
        value = parts[near, :share, :].astype(F32) + parts[far, share : 2 * share, :].astype(F32)
        out[target, :share, :] = value.astype(BF16)
        for rank in range(ranks):
            out[target, share + rank * extra : share + (rank + 1) * extra, :] = parts[
                rank, 2 * share :, :
            ]


def depth_part(pos, parts, share, depth):
    ranks, height, width = parts.shape
    shape = (depth, share + ranks * (height - 2 * share), width)

    def kernel(*refs):
        depth_kernel(share, *refs)

    return pl.pallas_call(
        kernel,
        out_shape=shape_of(shape),
        in_specs=[SMEM, VMEM],
        out_specs=VMEM,
        compiler_params=params(),
        cost_estimate=cost(parts.size, parts.size * 2 + math.prod(shape) * 2),
        name="depth_part",
    )(pos, parts)


def total_kernel(parts, out):
    total = parts[0].astype(F32)
    for source in range(1, parts.shape[0]):
        total += parts[source].astype(F32)
    out[...] = total.astype(BF16)


def total_part(parts):
    return pl.pallas_call(
        total_kernel,
        out_shape=shape_of(parts.shape[1:]),
        in_specs=[VMEM],
        out_specs=VMEM,
        compiler_params=params(),
        cost_estimate=cost(parts.size, parts.size * 2),
        name="total_part",
    )(parts)


def finish_kernel(ranks, scale, pos, pair, term, grads):
    width = pair.shape[2]
    own = grads.shape[0]
    start = pl.multiple_of(pos[3] * own, own)
    for core in (0, 1):
        side = slice(core * width, (core + 1) * width)
        grads[:, side] = pair[core, pl.ds(start, own), :]
    chunk = width // ranks
    for core in (0, 1):
        for rank in range(ranks):
            row = core * width + rank * chunk
            for side in (0, 1):
                first = 2 * own + (2 * rank + side) * chunk
                value = pair[core, first : first + chunk, :].astype(F32) / scale
                term[row : row + chunk, side * width : (side + 1) * width] = value


def finish_part(pos, pair, ranks, own, nodes):
    width = pair.shape[2]

    def kernel(*refs):
        finish_kernel(ranks, math.sqrt(nodes), *refs)

    return pl.pallas_call(
        kernel,
        out_shape=(shape_of((2 * width, 2 * width), F32), shape_of((own, 2 * width))),
        in_specs=[SMEM, VMEM],
        out_specs=(VMEM, VMEM),
        compiler_params=params(),
        cost_estimate=cost(0, pair.size * 2),
        name="finish_part",
    )(pos, pair)


def exchange(pieces, axis):
    return lax.all_to_all(pieces, axis, split_axis=0, concat_axis=0, tiled=True)


def per_device(features, weight, cotangent, tile_values, tile_rows, tile_cols, tile_count):
    rows, columns = features.shape
    width = columns // 2
    depth, sections, ranks = lax.axis_size("z"), lax.axis_size("y"), lax.axis_size("x")
    nodes = rows * depth * sections
    own = rows // (2 * ranks)
    core = lax.axis_index("core")
    pos = jnp.stack(
        [lax.axis_index("z"), lax.axis_index("y"), lax.axis_index("x"), core]
    ).astype(jnp.int32)

    mine = dense_blocks(tile_values[0], tile_rows[0], tile_cols[0], tile_count[0], rows)
    other = lax.ppermute(mine, "core", [(0, 1), (1, 0)])

    share = rows // ranks
    corner = (lax.axis_index("x") * share, core * width)
    piece = lax.dynamic_slice(features, corner, (share, width))
    planes = exchange(jnp.broadcast_to(piece, (depth, share, width)), "z")
    blocks = exchange(window_pieces(pos, planes, sections, ranks), ("y", "x"))
    part = forward_part(pos, mine, other, blocks.reshape(sections, rows, width))
    parts = exchange(part.reshape(2 * ranks, own, width), ("x", "core"))
    activations, pieces = layer_part(parts, cotangent, weight)
    parts = exchange(pieces, ("x", "core"))
    pieces = exchange(backward_part(pos, parts, mine, other, own), "y")
    pieces = exchange(planes_part(pos, pieces, rows, ranks), "x")
    pieces = exchange(depth_part(pos, pieces, share, depth), "z")
    pair = lax.all_gather(total_part(pieces), "core", axis=0, tiled=False)
    weight_grad, feature_grad = finish_part(pos, pair, ranks, own, nodes)
    return (activations, weight_grad, feature_grad)


def solution(mesh):
    blk, rep = mesh.devices.shape
    ranks = rep // 2
    devices = mesh.devices.reshape(ranks, blk // ranks, ranks, 2)
    grid = Mesh(devices, ("z", "y", "x", "core"))
    blk_axes, rep_axes = ("z", "y"), ("x", "core")
    return jax.shard_map(
        per_device,
        mesh=grid,
        in_specs=(
            P(blk_axes, None),
            P(),
            P(blk_axes + rep_axes, None),
            P(blk_axes, rep_axes, None, None, None),
            P(blk_axes, rep_axes, None),
            P(blk_axes, rep_axes, None),
            P(blk_axes, rep_axes),
        ),
        out_specs=(P(blk_axes + rep_axes, None), P(), P(blk_axes + rep_axes, None)),
        check_vma=False,
    )
```

```python
import math

import jax
import jax.numpy as jnp
from jax import lax
from jax.experimental import pallas as pl
from jax.experimental.pallas import tpu as pltpu
from jax.sharding import Mesh
from jax.sharding import PartitionSpec as P

TILE = 128
BF16 = jnp.bfloat16
F32 = jnp.float32
VMEM = pl.BlockSpec(memory_space=pltpu.VMEM)
SMEM = pl.BlockSpec(memory_space=pltpu.SMEM)
ANY = pl.BlockSpec(memory_space=pl.ANY)


def params(mib=40):
    return pltpu.CompilerParams(vmem_limit_bytes=mib << 20)


def shape_of(shape, dtype=BF16):
    return jax.ShapeDtypeStruct(shape, dtype)


def cost(flops, nbytes):
    return pl.CostEstimate(flops=flops, bytes_accessed=nbytes, transcendentals=0)


def dense_kernel(rows, cols, count, tiles, out):
    section = pl.program_id(0)
    out[...] = jnp.zeros_like(out)
    for slot in range(tiles.shape[1]):

        @pl.when(slot < count[section])
        def _():
            row = pl.multiple_of(rows[section, slot] * TILE, TILE)
            col = pl.multiple_of(cols[section, slot] * TILE, TILE)
            out[pl.ds(row, TILE), pl.ds(col, TILE)] = tiles[0, slot]


def dense_blocks(tiles, rows, cols, count, rows_blk):
    sections, slots = tiles.shape[:2]
    return pl.pallas_call(
        dense_kernel,
        grid=(sections,),
        out_shape=shape_of((rows_blk, sections * rows_blk)),
        in_specs=[
            SMEM,
            SMEM,
            SMEM,
            pl.BlockSpec((1, slots, TILE, TILE), lambda i: (i, 0, 0, 0)),
        ],
        out_specs=pl.BlockSpec((rows_blk, rows_blk), lambda i: (0, i)),
        compiler_params=params(),
        cost_estimate=cost(0, tiles.size * 2 + sections * rows_blk * rows_blk * 2),
        name="dense_blocks",
    )(rows, cols, count, tiles)


def light_kernel(pos, planes, out):
    ranks, share = planes.shape[:2]
    first = pos[0] + pos[2]
    for target in range(ranks):
        ahead = ((target > pos[1]) & (pos[3] == 1)).astype(jnp.int32)
        out[target, :share, :] = planes[lax.rem(first + ahead, ranks)]
        out[target, share:, :] = planes[lax.rem(first + 1, ranks)]


def light_pieces(pos, planes):
    ranks, share, width = planes.shape
    shape = (ranks, 2 * share, width)
    return pl.pallas_call(
        light_kernel,
        out_shape=shape_of(shape),
        in_specs=[SMEM, VMEM],
        out_specs=VMEM,
        compiler_params=params(),
        cost_estimate=cost(0, math.prod(shape) * 2),
        name="light_pieces",
    )(pos, planes)


def heavy_kernel(pos, parts, out):
    ranks = parts.shape[0]
    share = parts.shape[1] // 2
    for target in range(ranks):
        ahead = ((target > pos[1]) & (pos[3] == 0)).astype(jnp.int32)
        start = pl.multiple_of(ahead * share, share)
        for rank in range(ranks):
            out[target, rank] = parts[rank, pl.ds(start, share), :]


def heavy_pieces(pos, parts):
    ranks, height, width = parts.shape
    shape = (ranks, ranks, height // 2, width)
    return pl.pallas_call(
        heavy_kernel,
        out_shape=shape_of(shape),
        in_specs=[SMEM, VMEM],
        out_specs=VMEM,
        compiler_params=params(),
        cost_estimate=cost(0, math.prod(shape) * 2),
        name="heavy_pieces",
    )(pos, parts)


def block_order(pos, sections, own, section):
    core = pos[3] if own else 1 - pos[3]
    return lax.rem(pos[1] + core * (sections // 2) + section, sections)


def forward_kernel(pos, mine, other, parts, out, held, sem):
    copy = pltpu.make_async_copy(other, held, sem)
    copy.start()
    ranks = parts.shape[0]
    flip = pos[3]
    turned = None
    for is_own, matrix in ((True, mine), (False, held)):
        slices = []
        for section in range(ranks // 2):
            block = block_order(pos, ranks, is_own, section)
            for rank in range(ranks):
                outer = jnp.where(flip == 0, block, rank)
                inner = jnp.where(flip == 0, rank, block)
                slices.append(parts[outer, inner])
        if not is_own:
            copy.wait()
        product = lax.dot_general(
            jnp.concatenate(slices, axis=0).T,
            matrix[...],
            (((1,), (1,)), ((), ())),
            preferred_element_type=F32,
        )
        turned = product if turned is None else turned + product
    out[...] = turned.astype(BF16).T


def forward_part(pos, mine, other, parts):
    rows, columns = mine.shape
    width = parts.shape[-1]
    return pl.pallas_call(
        forward_kernel,
        out_shape=shape_of((rows, width)),
        in_specs=[SMEM, VMEM, ANY, VMEM],
        out_specs=VMEM,
        scratch_shapes=[pltpu.VMEM(other.shape, BF16), pltpu.SemaphoreType.DMA],
        compiler_params=params(),
        cost_estimate=cost(4 * rows * columns * width, 4 * rows * columns + parts.size * 2),
        name="forward_part",
    )(pos, mine, other, parts)


def layer_kernel(pos, parts, cot, weight, act, out, term):
    replicas, own, width = parts.shape
    ranks = replicas // 2
    sides = []
    for core in (0, 1):
        side = parts[core].astype(F32)
        for rank in range(1, ranks):
            side += parts[2 * rank + core].astype(F32)
        sides.append(side)
    agg = jnp.concatenate(sides, axis=1).astype(BF16)
    z_value = jnp.dot(agg, weight[...], preferred_element_type=F32)
    sigma = jax.nn.sigmoid(z_value)
    act[...] = (z_value * sigma).astype(BF16)
    slope = cot[...].astype(F32) * sigma * (1.0 + z_value * (1.0 - sigma))
    dz_value = slope.astype(BF16)
    dy_value = lax.dot_general(
        dz_value, weight[...], (((1,), (1,)), ((), ())), preferred_element_type=F32
    ).astype(BF16)
    term[...] = lax.dot_general(
        agg, dz_value, (((0,), (0,)), ((), ())), preferred_element_type=F32
    ).astype(BF16)
    chunk = width // ranks
    for rank in range(ranks):
        for core in (0, 1):
            target = 2 * rank + core
            row = core * width + lax.rem(pos[0] + rank, ranks) * chunk
            piece = term[pl.ds(pl.multiple_of(row, chunk), chunk), :]
            out[target, :own, :] = dy_value[:, core * width : (core + 1) * width]
            out[target, own : own + chunk, :] = piece[:, :width]
            out[target, own + chunk :, :] = piece[:, width:]


def layer_part(pos, parts, cot, weight):
    replicas, own, width = parts.shape
    out = (replicas, own + 4 * width // replicas, width)
    return pl.pallas_call(
        layer_kernel,
        out_shape=(shape_of(cot.shape), shape_of(out)),
        in_specs=[SMEM, VMEM, VMEM, VMEM],
        out_specs=(VMEM, VMEM),
        scratch_shapes=[pltpu.VMEM(weight.shape, BF16)],
        compiler_params=params(),
        cost_estimate=cost(6 * own * 4 * width * width, math.prod(out) * 4),
        name="layer_part",
    )(pos, parts, cot, weight)


def backward_kernel(own, pos, parts, mine, other, out, held, sem):
    copy = pltpu.make_async_copy(other, held, sem)
    copy.start()
    replicas, _, width = parts.shape
    ranks = replicas // 2
    rows = replicas * own
    share = rows // ranks
    piece = parts[0, own:, :].astype(F32)
    for source in range(1, replicas):
        piece += parts[source, own:, :].astype(F32)
    piece = piece.astype(BF16)
    for target in range(ranks):
        out[target, rows:, :] = piece
    dy_turned = parts[:, :own, :].reshape(rows, width).T
    flip = pos[3]
    for is_own, matrix in ((True, mine), (False, held)):
        if not is_own:
            copy.wait()
        for section in range(ranks // 2):
            side = matrix[:, section * rows : (section + 1) * rows]
            grads = jnp.dot(dy_turned, side, preferred_element_type=F32).astype(BF16).T
            block = block_order(pos, ranks, is_own, section)
            for rank in range(ranks):
                outer = jnp.where(flip == 0, block, rank)
                inner = jnp.where(flip == 0, rank, block)
                start = pl.multiple_of(inner * share, share)
                out[outer, pl.ds(start, share), :] = grads[rank * share : (rank + 1) * share, :]


def backward_part(pos, parts, mine, other, own):
    replicas, height, width = parts.shape
    rows, columns = mine.shape
    out = (replicas // 2, rows + height - own, width)

    def kernel(*refs):
        backward_kernel(own, *refs)

    return pl.pallas_call(
        kernel,
        out_shape=shape_of(out),
        in_specs=[SMEM, VMEM, VMEM, ANY],
        out_specs=VMEM,
        scratch_shapes=[pltpu.VMEM(other.shape, BF16), pltpu.SemaphoreType.DMA],
        compiler_params=params(),
        cost_estimate=cost(4 * rows * columns * width, 4 * rows * columns + math.prod(out) * 2),
        name="backward_part",
    )(pos, parts, mine, other)


def merge_kernel(rows, pos, parts, out):
    ranks, height, width = parts.shape
    share = rows // ranks
    term = parts[0, rows:, :].astype(F32)
    for source in range(1, ranks):
        term += parts[source, rows:, :].astype(F32)
    term = term.astype(BF16)
    for target in range(ranks):
        near = jnp.zeros((share, width), F32)
        far = near
        for source in range(ranks):
            value = parts[source, target * share : (target + 1) * share, :].astype(F32)
            same = (source <= pos[1]) | (pos[3] == 1)
            near += jnp.where(same, value, 0.0)
            far += jnp.where(same, 0.0, value)
        out[target, :share, :] = near.astype(BF16)
        out[target, share : 2 * share, :] = far.astype(BF16)
        out[target, 2 * share :, :] = term


def merge_part(pos, parts, rows):
    ranks, height, width = parts.shape
    shape = (ranks, 2 * rows // ranks + height - rows, width)

    def kernel(*refs):
        merge_kernel(rows, *refs)

    return pl.pallas_call(
        kernel,
        out_shape=shape_of(shape),
        in_specs=[SMEM, VMEM],
        out_specs=VMEM,
        compiler_params=params(),
        cost_estimate=cost(parts.size * 2, parts.size * 2 + math.prod(shape) * 2),
        name="merge_part",
    )(pos, parts)


def place_kernel(share, pos, parts, out):
    ranks, height, width = parts.shape
    own = share // 2
    near = jnp.zeros((share, width), F32)
    far = near
    term = jnp.zeros((height - 2 * share, width), F32)
    for source in range(ranks):
        first = parts[source, :share, :].astype(F32)
        second = parts[source, share : 2 * share, :].astype(F32)
        same = (source <= pos[1]) | (pos[3] == 0)
        near += jnp.where(same, first, 0.0)
        far += jnp.where(same, second, first)
        term += parts[source, 2 * share :, :].astype(F32)
    near, far, term = near.astype(BF16), far.astype(BF16), term.astype(BF16)
    plane = lax.rem(pos[0] + pos[2], ranks)
    behind = lax.rem(pos[0] + pos[2] + 1, ranks)
    nothing = jnp.zeros_like(near)
    for target in range(ranks):
        value = jnp.where(plane == target, near, jnp.where(behind == target, far, nothing))
        for core in (0, 1):
            out[2 * target + core, :own, :] = value[core * own : (core + 1) * own, :]
            out[2 * target + core, own:, :] = term


def place_part(pos, parts, share):
    ranks, height, width = parts.shape
    shape = (2 * ranks, height - 3 * share // 2, width)

    def kernel(*refs):
        place_kernel(share, *refs)

    return pl.pallas_call(
        kernel,
        out_shape=shape_of(shape),
        in_specs=[SMEM, VMEM],
        out_specs=VMEM,
        compiler_params=params(),
        cost_estimate=cost(parts.size, parts.size * 2 + math.prod(shape) * 2),
        name="place_part",
    )(pos, parts)


def finish_kernel(scale, pos, parts, term, grads):
    replicas, height, width = parts.shape
    ranks = replicas // 2
    own = grads.shape[0]
    chunk = width // ranks
    for core in (0, 1):
        total = parts[core, :own, :].astype(F32)
        for depth in range(1, ranks):
            total += parts[2 * depth + core, :own, :].astype(F32)
        grads[:, core * width : (core + 1) * width] = total.astype(BF16)
        for depth in range(ranks):
            row = core * width + lax.rem(pos[2] + depth, ranks) * chunk
            for side in (0, 1):
                first = own + side * chunk
                value = parts[2 * depth + core, first : first + chunk, :].astype(F32) / scale
                term[pl.ds(pl.multiple_of(row, chunk), chunk), side * width : (side + 1) * width] = value


def finish_part(pos, parts, own, nodes):
    width = parts.shape[2]

    def kernel(*refs):
        finish_kernel(math.sqrt(nodes), *refs)

    return pl.pallas_call(
        kernel,
        out_shape=(shape_of((2 * width, 2 * width), F32), shape_of((own, 2 * width))),
        in_specs=[SMEM, VMEM],
        out_specs=(VMEM, VMEM),
        compiler_params=params(),
        cost_estimate=cost(parts.size, parts.size * 2),
        name="finish_part",
    )(pos, parts)


def device_at(ranks, depth, section, rank, core):
    return ((depth % ranks * ranks + section) * ranks + rank) * 2 + core


def groups(ranks, kinds):
    found = []
    for core, kind in enumerate(kinds):
        for a in range(ranks):
            for b in range(ranks):
                if kind == "line":
                    found.append([device_at(ranks, a, k, b, core) for k in range(ranks)])
                else:
                    found.append([device_at(ranks, a - k, b, k, core) for k in range(ranks)])
    return found


def grouped(pieces, ranks, kinds):
    return lax.all_to_all(
        pieces,
        ("z", "y", "x", "core"),
        split_axis=0,
        concat_axis=0,
        axis_index_groups=groups(ranks, kinds),
        tiled=True,
    )


def exchange(pieces, axis):
    return lax.all_to_all(pieces, axis, split_axis=0, concat_axis=0, tiled=True)


def per_device(features, weight, cotangent, tile_values, tile_rows, tile_cols, tile_count):
    rows, columns = features.shape
    width = columns // 2
    ranks = lax.axis_size("x")
    share = rows // ranks
    own = share // 2
    core = lax.axis_index("core")
    pos = jnp.stack(
        [lax.axis_index("z"), lax.axis_index("y"), lax.axis_index("x"), core]
    ).astype(jnp.int32)

    mine = dense_blocks(tile_values[0], tile_rows[0], tile_cols[0], tile_count[0], rows)
    other = lax.ppermute(mine, "core", [(0, 1), (1, 0)])

    corner = (lax.axis_index("x") * share, core * width)
    piece = lax.dynamic_slice(features, corner, (share, width))
    planes = exchange(jnp.broadcast_to(piece, (ranks, share, width)), "z")
    parts = grouped(light_pieces(pos, planes), ranks, ("diagonal", "line"))
    parts = grouped(heavy_pieces(pos, parts), ranks, ("line", "diagonal"))
    part = forward_part(pos, mine, other, parts)
    parts = exchange(part.reshape(2 * ranks, own, width), ("x", "core"))
    activations, pieces = layer_part(pos, parts, cotangent, weight)
    parts = exchange(pieces, ("x", "core"))
    pieces = backward_part(pos, parts, mine, other, own)
    parts = grouped(pieces, ranks, ("line", "diagonal"))
    parts = grouped(merge_part(pos, parts, rows), ranks, ("diagonal", "line"))
    parts = exchange(place_part(pos, parts, share), ("z", "core"))
    weight_grad, feature_grad = finish_part(pos, parts, own, rows * ranks * ranks)
    return (activations, weight_grad, feature_grad)


def solution(mesh):
    blk, rep = mesh.devices.shape
    ranks = rep // 2
    devices = mesh.devices.reshape(ranks, blk // ranks, ranks, 2)
    grid = Mesh(devices, ("z", "y", "x", "core"))
    blk_axes, rep_axes = ("z", "y"), ("x", "core")
    return jax.shard_map(
        per_device,
        mesh=grid,
        in_specs=(
            P(blk_axes, None),
            P(),
            P(blk_axes + rep_axes, None),
            P(blk_axes, rep_axes, None, None, None),
            P(blk_axes, rep_axes, None),
            P(blk_axes, rep_axes, None),
            P(blk_axes, rep_axes),
        ),
        out_specs=(P(blk_axes + rep_axes, None), P(), P(blk_axes + rep_axes, None)),
        check_vma=False,
    )
```

```python
import math

import jax
import jax.numpy as jnp
from jax import lax
from jax.experimental import pallas as pl
from jax.experimental.pallas import tpu as pltpu
from jax.sharding import Mesh
from jax.sharding import PartitionSpec as P

TILE = 128
BF16 = jnp.bfloat16
F32 = jnp.float32
VMEM = pl.BlockSpec(memory_space=pltpu.VMEM)
SMEM = pl.BlockSpec(memory_space=pltpu.SMEM)
ANY = pl.BlockSpec(memory_space=pl.ANY)


def params(mib=40):
    return pltpu.CompilerParams(vmem_limit_bytes=mib << 20)


def shape_of(shape, dtype=BF16):
    return jax.ShapeDtypeStruct(shape, dtype)


def cost(flops, nbytes):
    return pl.CostEstimate(flops=flops, bytes_accessed=nbytes, transcendentals=0)


def wrap(index, size):
    return jnp.where(index >= size, index - size, index)


def dense_kernel(rows, cols, count, tiles, out):
    sections, slots = tiles.shape[:2]
    span = out.shape[0]
    for section in range(sections):
        out[:, section * span : (section + 1) * span] = jnp.zeros((span, span), BF16)
        for slot in range(slots):

            @pl.when(slot < count[section])
            def _():
                row = pl.multiple_of(rows[section, slot] * TILE, TILE)
                col = pl.multiple_of(section * span + cols[section, slot] * TILE, TILE)
                out[pl.ds(row, TILE), pl.ds(col, TILE)] = tiles[section, slot]


def dense_blocks(tiles, rows, cols, count, rows_blk):
    sections = tiles.shape[0]
    shape = (rows_blk, sections * rows_blk)
    return pl.pallas_call(
        dense_kernel,
        out_shape=shape_of(shape),
        in_specs=[SMEM, SMEM, SMEM, VMEM],
        out_specs=VMEM,
        compiler_params=params(),
        cost_estimate=cost(0, tiles.size * 2 + math.prod(shape) * 2),
        name="dense_blocks",
    )(rows, cols, count, tiles)


def window_kernel(pos, planes, out):
    ranks = planes.shape[0]
    plane = [pos[0]]
    for step in range(ranks):
        plane.append(wrap(plane[-1] + 1, ranks))
    for target in range(out.shape[0]):
        section, rank = target // ranks, target % ranks
        out[target] = planes[jnp.where(section > pos[1], plane[rank + 1], plane[rank])]


def window_pieces(pos, planes, sections):
    ranks = planes.shape[0]
    shape = (sections * ranks,) + planes.shape[1:]
    return pl.pallas_call(
        window_kernel,
        out_shape=shape_of(shape),
        in_specs=[SMEM, VMEM],
        out_specs=VMEM,
        compiler_params=params(),
        cost_estimate=cost(0, math.prod(shape) * 2),
        name="window_pieces",
    )(pos, planes)


def block_order(pos, sections, own, section):
    core = pos[3] if own else 1 - pos[3]
    return wrap(pos[1] + core * (sections // 2) + section, sections)


def forward_kernel(pos, mine, other, blocks, out, held, sem):
    copy = pltpu.make_async_copy(other, held, sem)
    copy.start()
    sections = blocks.shape[0]
    total = None
    for is_own, matrix in ((True, mine), (False, held)):
        side = jnp.concatenate(
            [blocks[block_order(pos, sections, is_own, i)] for i in range(sections // 2)], axis=0
        )
        if not is_own:
            copy.wait()
        product = jnp.dot(matrix[...], side, preferred_element_type=F32)
        total = product if total is None else total + product
    out[...] = total.astype(BF16)


def forward_part(pos, mine, other, blocks):
    rows, columns = mine.shape
    width = blocks.shape[-1]
    return pl.pallas_call(
        forward_kernel,
        out_shape=shape_of((rows, width)),
        in_specs=[SMEM, VMEM, ANY, VMEM],
        out_specs=VMEM,
        scratch_shapes=[pltpu.VMEM(other.shape, BF16), pltpu.SemaphoreType.DMA],
        compiler_params=params(),
        cost_estimate=cost(4 * rows * columns * width, 4 * rows * columns + blocks.size * 2),
        name="forward_part",
    )(pos, mine, other, blocks)


def layer_kernel(pos, parts, cot, weight, act, out, term):
    replicas, own, width = parts.shape
    ranks = replicas // 2
    sides = []
    for core in (0, 1):
        side = parts[core].astype(F32)
        for rank in range(1, ranks):
            side += parts[2 * rank + core].astype(F32)
        sides.append(side)
    agg = jnp.concatenate(sides, axis=1).astype(BF16)
    z_value = jnp.dot(agg, weight[...], preferred_element_type=F32)
    sigma = jax.nn.sigmoid(z_value)
    act[...] = (z_value * sigma).astype(BF16)
    slope = cot[...].astype(F32) * sigma * (1.0 + z_value * (1.0 - sigma))
    dz_value = slope.astype(BF16)
    dy_value = lax.dot_general(
        dz_value, weight[...], (((1,), (1,)), ((), ())), preferred_element_type=F32
    ).astype(BF16)
    term[...] = lax.dot_general(
        agg, dz_value, (((0,), (0,)), ((), ())), preferred_element_type=F32
    ).astype(BF16)
    chunk = width // ranks
    for rank in range(ranks):
        for core in (0, 1):
            target = 2 * rank + core
            row = core * width + wrap(pos[0] + rank, ranks) * chunk
            piece = term[pl.ds(pl.multiple_of(row, chunk), chunk), :]
            out[target, :own, :] = dy_value[:, core * width : (core + 1) * width]
            out[target, own : own + chunk, :] = piece[:, :width]
            out[target, own + chunk :, :] = piece[:, width:]


def layer_part(pos, parts, cot, weight):
    replicas, own, width = parts.shape
    out = (replicas, own + 4 * width // replicas, width)
    return pl.pallas_call(
        layer_kernel,
        out_shape=(shape_of(cot.shape), shape_of(out)),
        in_specs=[SMEM, VMEM, VMEM, VMEM],
        out_specs=(VMEM, VMEM),
        scratch_shapes=[pltpu.VMEM(weight.shape, BF16)],
        compiler_params=params(),
        cost_estimate=cost(6 * own * 4 * width * width, math.prod(out) * 4),
        name="layer_part",
    )(pos, parts, cot, weight)


def backward_kernel(own, pos, parts, mine, other, out, held, sem):
    copy = pltpu.make_async_copy(other, held, sem)
    copy.start()
    replicas, _, width = parts.shape
    ranks = replicas // 2
    rows = replicas * own
    share = rows // ranks
    piece = parts[0, own:, :].astype(F32)
    for source in range(1, replicas):
        piece += parts[source, own:, :].astype(F32)
    piece = piece.astype(BF16)
    for target in range(ranks):
        out[target, rows:, :] = piece
    dy_turned = parts[:, :own, :].reshape(rows, width).T
    flip = pos[3]
    for is_own, matrix in ((True, mine), (False, held)):
        if not is_own:
            copy.wait()
        for section in range(ranks // 2):
            side = matrix[:, section * rows : (section + 1) * rows]
            grads = jnp.dot(dy_turned, side, preferred_element_type=F32).astype(BF16).T
            block = block_order(pos, ranks, is_own, section)
            for rank in range(ranks):
                outer = jnp.where(flip == 0, block, rank)
                inner = jnp.where(flip == 0, rank, block)
                start = pl.multiple_of(inner * share, share)
                out[outer, pl.ds(start, share), :] = grads[rank * share : (rank + 1) * share, :]


def backward_part(pos, parts, mine, other, own):
    replicas, height, width = parts.shape
    rows, columns = mine.shape
    out = (replicas // 2, rows + height - own, width)

    def kernel(*refs):
        backward_kernel(own, *refs)

    return pl.pallas_call(
        kernel,
        out_shape=shape_of(out),
        in_specs=[SMEM, VMEM, VMEM, ANY],
        out_specs=VMEM,
        scratch_shapes=[pltpu.VMEM(other.shape, BF16), pltpu.SemaphoreType.DMA],
        compiler_params=params(),
        cost_estimate=cost(4 * rows * columns * width, 4 * rows * columns + math.prod(out) * 2),
        name="backward_part",
    )(pos, parts, mine, other)


def merge_kernel(rows, pos, parts, out):
    ranks, height, width = parts.shape
    share = rows // ranks
    term = parts[0, rows:, :].astype(F32)
    for source in range(1, ranks):
        term += parts[source, rows:, :].astype(F32)
    term = term.astype(BF16)
    for target in range(ranks):
        near = jnp.zeros((share, width), F32)
        far = near
        for source in range(ranks):
            value = parts[source, target * share : (target + 1) * share, :].astype(F32)
            same = (source <= pos[1]) | (pos[3] == 1)
            near += jnp.where(same, value, 0.0)
            far += jnp.where(same, 0.0, value)
        out[target, :share, :] = near.astype(BF16)
        out[target, share : 2 * share, :] = far.astype(BF16)
        out[target, 2 * share :, :] = term


def merge_part(pos, parts, rows):
    ranks, height, width = parts.shape
    shape = (ranks, 2 * rows // ranks + height - rows, width)

    def kernel(*refs):
        merge_kernel(rows, *refs)

    return pl.pallas_call(
        kernel,
        out_shape=shape_of(shape),
        in_specs=[SMEM, VMEM],
        out_specs=VMEM,
        compiler_params=params(),
        cost_estimate=cost(parts.size * 2, parts.size * 2 + math.prod(shape) * 2),
        name="merge_part",
    )(pos, parts)


def place_kernel(share, pos, parts, out):
    ranks, height, width = parts.shape
    own = share // 2
    near = jnp.zeros((share, width), F32)
    far = near
    term = jnp.zeros((height - 2 * share, width), F32)
    for source in range(ranks):
        first = parts[source, :share, :].astype(F32)
        second = parts[source, share : 2 * share, :].astype(F32)
        same = (source <= pos[1]) | (pos[3] == 0)
        near += jnp.where(same, first, 0.0)
        far += jnp.where(same, second, first)
        term += parts[source, 2 * share :, :].astype(F32)
    near, far, term = near.astype(BF16), far.astype(BF16), term.astype(BF16)
    plane = wrap(pos[0] + pos[2], ranks)
    behind = wrap(plane + 1, ranks)
    nothing = jnp.zeros_like(near)
    for target in range(ranks):
        value = jnp.where(plane == target, near, jnp.where(behind == target, far, nothing))
        for core in (0, 1):
            out[2 * target + core, :own, :] = value[core * own : (core + 1) * own, :]
            out[2 * target + core, own:, :] = term


def place_part(pos, parts, share):
    ranks, height, width = parts.shape
    shape = (2 * ranks, height - 3 * share // 2, width)

    def kernel(*refs):
        place_kernel(share, *refs)

    return pl.pallas_call(
        kernel,
        out_shape=shape_of(shape),
        in_specs=[SMEM, VMEM],
        out_specs=VMEM,
        compiler_params=params(),
        cost_estimate=cost(parts.size, parts.size * 2 + math.prod(shape) * 2),
        name="place_part",
    )(pos, parts)


def finish_kernel(scale, pos, parts, term, grads):
    replicas, height, width = parts.shape
    ranks = replicas // 2
    own = grads.shape[0]
    chunk = width // ranks
    for core in (0, 1):
        total = parts[core, :own, :].astype(F32)
        for depth in range(1, ranks):
            total += parts[2 * depth + core, :own, :].astype(F32)
        grads[:, core * width : (core + 1) * width] = total.astype(BF16)
        for depth in range(ranks):
            row = core * width + wrap(pos[2] + depth, ranks) * chunk
            for side in (0, 1):
                first = own + side * chunk
                value = parts[2 * depth + core, first : first + chunk, :].astype(F32) / scale
                term[pl.ds(pl.multiple_of(row, chunk), chunk), side * width : (side + 1) * width] = value


def finish_part(pos, parts, own, nodes):
    width = parts.shape[2]

    def kernel(*refs):
        finish_kernel(math.sqrt(nodes), *refs)

    return pl.pallas_call(
        kernel,
        out_shape=(shape_of((2 * width, 2 * width), F32), shape_of((own, 2 * width))),
        in_specs=[SMEM, VMEM],
        out_specs=(VMEM, VMEM),
        compiler_params=params(),
        cost_estimate=cost(parts.size, parts.size * 2),
        name="finish_part",
    )(pos, parts)


def device_at(ranks, depth, section, rank, core):
    return ((depth % ranks * ranks + section) * ranks + rank) * 2 + core


def groups(ranks, kinds):
    found = []
    for core, kind in enumerate(kinds):
        for a in range(ranks):
            for b in range(ranks):
                if kind == "line":
                    found.append([device_at(ranks, a, k, b, core) for k in range(ranks)])
                else:
                    found.append([device_at(ranks, a - k, b, k, core) for k in range(ranks)])
    return found


def grouped(pieces, ranks, kinds):
    return lax.all_to_all(
        pieces,
        ("z", "y", "x", "core"),
        split_axis=0,
        concat_axis=0,
        axis_index_groups=groups(ranks, kinds),
        tiled=True,
    )


def exchange(pieces, axis):
    return lax.all_to_all(pieces, axis, split_axis=0, concat_axis=0, tiled=True)


def per_device(features, weight, cotangent, tile_values, tile_rows, tile_cols, tile_count):
    rows, columns = features.shape
    width = columns // 2
    ranks = lax.axis_size("x")
    share = rows // ranks
    own = share // 2
    pos = jnp.stack([lax.axis_index(name) for name in ("z", "y", "x", "core")]).astype(jnp.int32)

    mine = dense_blocks(tile_values[0], tile_rows[0], tile_cols[0], tile_count[0], rows)
    other = lax.ppermute(mine, "core", [(0, 1), (1, 0)])

    corner = (lax.axis_index("x") * share, lax.axis_index("core") * width)
    piece = lax.dynamic_slice(features, corner, (share, width))
    planes = exchange(jnp.broadcast_to(piece, (ranks, share, width)), "z")
    blocks = exchange(window_pieces(pos, planes, ranks), ("y", "x"))
    part = forward_part(pos, mine, other, blocks.reshape(ranks, rows, width))
    parts = exchange(part.reshape(2 * ranks, own, width), ("x", "core"))
    activations, pieces = layer_part(pos, parts, cotangent, weight)
    parts = exchange(pieces, ("x", "core"))
    pieces = backward_part(pos, parts, mine, other, own)
    parts = grouped(pieces, ranks, ("line", "diagonal"))
    parts = grouped(merge_part(pos, parts, rows), ranks, ("diagonal", "line"))
    parts = exchange(place_part(pos, parts, share), ("z", "core"))
    weight_grad, feature_grad = finish_part(pos, parts, own, rows * ranks * ranks)
    return (activations, weight_grad, feature_grad)


def solution(mesh):
    blk, rep = mesh.devices.shape
    ranks = rep // 2
    devices = mesh.devices.reshape(ranks, blk // ranks, ranks, 2)
    grid = Mesh(devices, ("z", "y", "x", "core"))
    blk_axes, rep_axes = ("z", "y"), ("x", "core")
    return jax.shard_map(
        per_device,
        mesh=grid,
        in_specs=(
            P(blk_axes, None),
            P(),
            P(blk_axes + rep_axes, None),
            P(blk_axes, rep_axes, None, None, None),
            P(blk_axes, rep_axes, None),
            P(blk_axes, rep_axes, None),
            P(blk_axes, rep_axes),
        ),
        out_specs=(P(blk_axes + rep_axes, None), P(), P(blk_axes + rep_axes, None)),
        check_vma=False,
    )
```

```python
import math

import jax
import jax.numpy as jnp
from jax import lax
from jax.experimental import pallas as pl
from jax.experimental.pallas import tpu as pltpu
from jax.sharding import Mesh
from jax.sharding import PartitionSpec as P

TILE = 128
BF16 = jnp.bfloat16
F32 = jnp.float32
VMEM = pl.BlockSpec(memory_space=pltpu.VMEM)
SMEM = pl.BlockSpec(memory_space=pltpu.SMEM)
ANY = pl.BlockSpec(memory_space=pl.ANY)


def params(mib=40):
    return pltpu.CompilerParams(vmem_limit_bytes=mib << 20)


def shape_of(shape, dtype=BF16):
    return jax.ShapeDtypeStruct(shape, dtype)


def cost(flops, nbytes):
    return pl.CostEstimate(flops=flops, bytes_accessed=nbytes, transcendentals=0)


def wrap(index, size):
    return jnp.where(index >= size, index - size, index)


def dense_kernel(index, tiles, out):
    sections, slots = tiles.shape[:2]
    span = out.shape[0]
    for section in range(sections):
        out[:, section * span : (section + 1) * span] = jnp.zeros((span, span), BF16)
        for slot in range(slots):

            @pl.when(slot < index[section, 2 * slots])
            def _():
                row = pl.multiple_of(index[section, slot] * TILE, TILE)
                col = pl.multiple_of(section * span + index[section, slots + slot] * TILE, TILE)
                out[pl.ds(row, TILE), pl.ds(col, TILE)] = tiles[section, slot]


def dense_blocks(tiles, rows, cols, count, rows_blk):
    sections = tiles.shape[0]
    shape = (rows_blk, sections * rows_blk)
    index = jnp.concatenate([rows, cols, count[:, None]], axis=1)
    return pl.pallas_call(
        dense_kernel,
        out_shape=shape_of(shape),
        in_specs=[SMEM, VMEM],
        out_specs=VMEM,
        compiler_params=params(),
        cost_estimate=cost(0, tiles.size * 2 + math.prod(shape) * 2),
        name="dense_blocks",
    )(index, tiles)


def window_kernel(pos, planes, out):
    ranks = planes.shape[0]
    place = [pos[2]]
    for step in range(ranks):
        place.append(wrap(place[-1] + 1, ranks))
    for target in range(out.shape[0]):
        section, step = target // ranks, target % ranks
        out[target] = planes[jnp.where(section > pos[1], place[step + 1], place[step])]


def window_pieces(pos, planes, sections):
    ranks = planes.shape[0]
    shape = (sections * ranks,) + planes.shape[1:]
    return pl.pallas_call(
        window_kernel,
        out_shape=shape_of(shape),
        in_specs=[SMEM, VMEM],
        out_specs=VMEM,
        compiler_params=params(),
        cost_estimate=cost(0, math.prod(shape) * 2),
        name="window_pieces",
    )(pos, planes)


def block_order(pos, sections, own, section):
    core = pos[3] if own else 1 - pos[3]
    return wrap(pos[1] + core * (sections // 2) + section, sections)


def forward_kernel(pos, mine, other, blocks, out, held, sem):
    copy = pltpu.make_async_copy(other, held, sem)
    copy.start()
    sections = blocks.shape[0]
    total = None
    for is_own, matrix in ((True, mine), (False, held)):
        side = jnp.concatenate(
            [blocks[block_order(pos, sections, is_own, i)] for i in range(sections // 2)], axis=0
        )
        if not is_own:
            copy.wait()
        product = jnp.dot(matrix[...], side, preferred_element_type=F32)
        total = product if total is None else total + product
    out[...] = total.astype(BF16)


def forward_part(pos, mine, other, blocks):
    rows, columns = mine.shape
    width = blocks.shape[-1]
    return pl.pallas_call(
        forward_kernel,
        out_shape=shape_of((rows, width)),
        in_specs=[SMEM, VMEM, ANY, VMEM],
        out_specs=VMEM,
        scratch_shapes=[pltpu.VMEM(other.shape, BF16), pltpu.SemaphoreType.DMA],
        compiler_params=params(),
        cost_estimate=cost(4 * rows * columns * width, 4 * rows * columns + blocks.size * 2),
        name="forward_part",
    )(pos, mine, other, blocks)


def layer_kernel(pos, parts, cot, weight, act, out, term):
    replicas, own, width = parts.shape
    ranks = replicas // 2
    sides = []
    for core in (0, 1):
        side = parts[core].astype(F32)
        for rank in range(1, ranks):
            side += parts[2 * rank + core].astype(F32)
        sides.append(side)
    agg = jnp.concatenate(sides, axis=1).astype(BF16)
    z_value = jnp.dot(agg, weight[...], preferred_element_type=F32)
    sigma = jax.nn.sigmoid(z_value)
    act[...] = (z_value * sigma).astype(BF16)
    slope = cot[...].astype(F32) * sigma * (1.0 + z_value * (1.0 - sigma))
    dz_value = slope.astype(BF16)
    dy_value = lax.dot_general(
        dz_value, weight[...], (((1,), (1,)), ((), ())), preferred_element_type=F32
    ).astype(BF16)
    term[...] = lax.dot_general(
        agg, dz_value, (((0,), (0,)), ((), ())), preferred_element_type=F32
    ).astype(BF16)
    chunk = width // ranks
    for rank in range(ranks):
        for core in (0, 1):
            target = 2 * rank + core
            row = core * width + wrap(pos[0] + rank, ranks) * chunk
            piece = term[pl.ds(pl.multiple_of(row, chunk), chunk), :]
            out[target, :own, :] = dy_value[:, core * width : (core + 1) * width]
            out[target, own : own + chunk, :] = piece[:, :width]
            out[target, own + chunk :, :] = piece[:, width:]


def layer_part(pos, parts, cot, weight):
    replicas, own, width = parts.shape
    out = (replicas, own + 4 * width // replicas, width)
    return pl.pallas_call(
        layer_kernel,
        out_shape=(shape_of(cot.shape), shape_of(out)),
        in_specs=[SMEM, VMEM, VMEM, VMEM],
        out_specs=(VMEM, VMEM),
        scratch_shapes=[pltpu.VMEM(weight.shape, BF16)],
        compiler_params=params(),
        cost_estimate=cost(6 * own * 4 * width * width, math.prod(out) * 4),
        name="layer_part",
    )(pos, parts, cot, weight)


def backward_kernel(own, pos, parts, mine, other, out, held, sem):
    copy = pltpu.make_async_copy(other, held, sem)
    copy.start()
    replicas, _, width = parts.shape
    ranks = replicas // 2
    rows = replicas * own
    share = rows // ranks
    piece = parts[0, own:, :].astype(F32)
    for source in range(1, replicas):
        piece += parts[source, own:, :].astype(F32)
    piece = piece.astype(BF16)
    height = out.shape[0] // ranks
    for target in range(ranks):
        out[target * height + rows : (target + 1) * height, :] = piece
    dy_turned = parts[:, :own, :].reshape(rows, width).T
    by_block = jnp.where(pos[3] == 0, height, share)
    by_rank = jnp.where(pos[3] == 0, share, height)
    for is_own, matrix in ((True, mine), (False, held)):
        if not is_own:
            copy.wait()
        for section in range(ranks // 2):
            side = matrix[:, section * rows : (section + 1) * rows]
            grads = jnp.dot(dy_turned, side, preferred_element_type=F32).astype(BF16).T
            first = block_order(pos, ranks, is_own, section) * by_block
            for rank in range(ranks):
                start = pl.multiple_of(first + rank * by_rank, 16)
                out[pl.ds(start, share), :] = grads[rank * share : (rank + 1) * share, :]


def backward_part(pos, parts, mine, other, own):
    replicas, height, width = parts.shape
    rows, columns = mine.shape
    out = (replicas // 2 * (rows + height - own), width)

    def kernel(*refs):
        backward_kernel(own, *refs)

    return pl.pallas_call(
        kernel,
        out_shape=shape_of(out),
        in_specs=[SMEM, VMEM, VMEM, ANY],
        out_specs=VMEM,
        scratch_shapes=[pltpu.VMEM(other.shape, BF16), pltpu.SemaphoreType.DMA],
        compiler_params=params(),
        cost_estimate=cost(4 * rows * columns * width, 4 * rows * columns + math.prod(out) * 2),
        name="backward_part",
    )(pos, parts, mine, other)


def merge_kernel(rows, pos, parts, out):
    ranks, height, width = parts.shape
    share = rows // ranks
    term = parts[0, rows:, :].astype(F32)
    for source in range(1, ranks):
        term += parts[source, rows:, :].astype(F32)
    term = term.astype(BF16)
    for target in range(ranks):
        near = jnp.zeros((share, width), F32)
        far = near
        for source in range(ranks):
            value = parts[source, target * share : (target + 1) * share, :].astype(F32)
            same = (source <= pos[1]) | (pos[3] == 1)
            near += jnp.where(same, value, 0.0)
            far += jnp.where(same, 0.0, value)
        out[target, :share, :] = near.astype(BF16)
        out[target, share : 2 * share, :] = far.astype(BF16)
        out[target, 2 * share :, :] = term


def merge_part(pos, parts, rows):
    ranks, height, width = parts.shape
    shape = (ranks, 2 * rows // ranks + height - rows, width)

    def kernel(*refs):
        merge_kernel(rows, *refs)

    return pl.pallas_call(
        kernel,
        out_shape=shape_of(shape),
        in_specs=[SMEM, VMEM],
        out_specs=VMEM,
        compiler_params=params(),
        cost_estimate=cost(parts.size * 2, parts.size * 2 + math.prod(shape) * 2),
        name="merge_part",
    )(pos, parts)


def place_kernel(share, pos, parts, out):
    ranks, height, width = parts.shape
    own = share // 2
    near = jnp.zeros((share, width), F32)
    far = near
    term = jnp.zeros((height - 2 * share, width), F32)
    for source in range(ranks):
        first = parts[source, :share, :].astype(F32)
        second = parts[source, share : 2 * share, :].astype(F32)
        same = (source <= pos[1]) | (pos[3] == 0)
        near += jnp.where(same, first, 0.0)
        far += jnp.where(same, second, first)
        term += parts[source, 2 * share :, :].astype(F32)
    near, far, term = near.astype(BF16), far.astype(BF16), term.astype(BF16)
    plane = wrap(pos[0] + pos[2], ranks)
    behind = wrap(plane + 1, ranks)
    nothing = jnp.zeros_like(near)
    for target in range(ranks):
        value = jnp.where(plane == target, near, jnp.where(behind == target, far, nothing))
        for core in (0, 1):
            out[2 * target + core, :own, :] = value[core * own : (core + 1) * own, :]
            out[2 * target + core, own:, :] = term


def place_part(pos, parts, share):
    ranks, height, width = parts.shape
    shape = (2 * ranks, height - 3 * share // 2, width)

    def kernel(*refs):
        place_kernel(share, *refs)

    return pl.pallas_call(
        kernel,
        out_shape=shape_of(shape),
        in_specs=[SMEM, VMEM],
        out_specs=VMEM,
        compiler_params=params(),
        cost_estimate=cost(parts.size, parts.size * 2 + math.prod(shape) * 2),
        name="place_part",
    )(pos, parts)


def finish_kernel(scale, pos, parts, term, grads):
    replicas, height, width = parts.shape
    ranks = replicas // 2
    own = grads.shape[0]
    chunk = width // ranks
    for core in (0, 1):
        total = parts[core, :own, :].astype(F32)
        for depth in range(1, ranks):
            total += parts[2 * depth + core, :own, :].astype(F32)
        grads[:, core * width : (core + 1) * width] = total.astype(BF16)
        for depth in range(ranks):
            row = core * width + wrap(pos[2] + depth, ranks) * chunk
            for side in (0, 1):
                first = own + side * chunk
                value = parts[2 * depth + core, first : first + chunk, :].astype(F32) / scale
                term[pl.ds(pl.multiple_of(row, chunk), chunk), side * width : (side + 1) * width] = value


def finish_part(pos, parts, own, nodes):
    width = parts.shape[2]

    def kernel(*refs):
        finish_kernel(math.sqrt(nodes), *refs)

    return pl.pallas_call(
        kernel,
        out_shape=(shape_of((2 * width, 2 * width), F32), shape_of((own, 2 * width))),
        in_specs=[SMEM, VMEM],
        out_specs=(VMEM, VMEM),
        compiler_params=params(),
        cost_estimate=cost(parts.size, parts.size * 2),
        name="finish_part",
    )(pos, parts)


def device_at(ranks, depth, section, rank, core):
    return ((depth % ranks * ranks + section) * ranks + rank) * 2 + core


def section_groups(ranks):
    every = [(a, b) for a in range(ranks) for b in range(ranks)]
    steps = range(ranks)
    line = [[device_at(ranks, a, k, b, 0) for k in steps] for a, b in every]
    slant = [[device_at(ranks, a - k, b, k, 1) for k in steps] for a, b in every]
    return line + slant


def share_groups(ranks):
    return [[device ^ 1 for device in group] for group in section_groups(ranks)]


def plane_groups(ranks):
    return [
        [device_at(ranks, i - rank, section, rank, core) for i in range(ranks)]
        for section in range(ranks)
        for rank in range(ranks)
        for core in (0, 1)
    ]


def window_groups(ranks):
    return [
        [
            device_at(ranks, depth, section, (i - depth) % ranks, core)
            for section in range(ranks)
            for i in range(ranks)
        ]
        for depth in range(ranks)
        for core in (0, 1)
    ]


def grouped(pieces, lists):
    return lax.all_to_all(
        pieces,
        ("z", "y", "x", "core"),
        split_axis=0,
        concat_axis=0,
        axis_index_groups=lists,
        tiled=True,
    )


def exchange(pieces, axis):
    return lax.all_to_all(pieces, axis, split_axis=0, concat_axis=0, tiled=True)


def per_device(features, weight, cotangent, tile_values, tile_rows, tile_cols, tile_count):
    rows, columns = features.shape
    width = columns // 2
    ranks = lax.axis_size("x")
    share = rows // ranks
    own = share // 2
    pos = jnp.stack([lax.axis_index(name) for name in ("z", "y", "x", "core")]).astype(jnp.int32)

    mine = dense_blocks(tile_values[0], tile_rows[0], tile_cols[0], tile_count[0], rows)
    other = lax.ppermute(mine, "core", [(0, 1), (1, 0)])

    half = lax.dynamic_slice_in_dim(features, lax.axis_index("core") * width, width, axis=1)
    planes = grouped(half.reshape(ranks, share, width), plane_groups(ranks))
    planes, other = lax.optimization_barrier((planes, other))
    blocks = grouped(window_pieces(pos, planes, ranks), window_groups(ranks))
    part = forward_part(pos, mine, other, blocks.reshape(ranks, rows, width))
    parts = exchange(part.reshape(2 * ranks, own, width), ("x", "core"))
    activations, pieces = layer_part(pos, parts, cotangent, weight)
    parts = exchange(pieces, ("x", "core"))
    pieces = backward_part(pos, parts, mine, other, own)
    parts = grouped(pieces, section_groups(ranks)).reshape(ranks, -1, width)
    parts = grouped(merge_part(pos, parts, rows), share_groups(ranks))
    parts = exchange(place_part(pos, parts, share), ("z", "core"))
    weight_grad, feature_grad = finish_part(pos, parts, own, rows * ranks * ranks)
    return (activations, weight_grad, feature_grad)


def solution(mesh):
    blk, rep = mesh.devices.shape
    ranks = rep // 2
    devices = mesh.devices.reshape(ranks, blk // ranks, ranks, 2)
    grid = Mesh(devices, ("z", "y", "x", "core"))
    blk_axes, rep_axes = ("z", "y"), ("x", "core")
    return jax.shard_map(
        per_device,
        mesh=grid,
        in_specs=(
            P(blk_axes, None),
            P(),
            P(blk_axes + rep_axes, None),
            P(blk_axes, rep_axes, None, None, None),
            P(blk_axes, rep_axes, None),
            P(blk_axes, rep_axes, None),
            P(blk_axes, rep_axes),
        ),
        out_specs=(P(blk_axes + rep_axes, None), P(), P(blk_axes + rep_axes, None)),
        check_vma=False,
    )
```

```python
import math

import jax
import jax.numpy as jnp
from jax import lax
from jax.experimental import pallas as pl
from jax.experimental.pallas import tpu as pltpu
from jax.sharding import Mesh
from jax.sharding import PartitionSpec as P

TILE = 128
BF16 = jnp.bfloat16
F32 = jnp.float32
VMEM = pl.BlockSpec(memory_space=pltpu.VMEM)
SMEM = pl.BlockSpec(memory_space=pltpu.SMEM)


def params(mib=40):
    return pltpu.CompilerParams(vmem_limit_bytes=mib << 20)


def shape_of(shape, dtype=BF16):
    return jax.ShapeDtypeStruct(shape, dtype)


def cost(flops, nbytes):
    return pl.CostEstimate(flops=flops, bytes_accessed=nbytes, transcendentals=0)


def wrap(index, size):
    return jnp.where(index >= size, index - size, index)


def dense_kernel(rows, cols, count, tiles, out):
    sections, slots = tiles.shape[:2]
    span = out.shape[0]
    for section in range(sections):
        out[:, section * span : (section + 1) * span] = jnp.zeros((span, span), BF16)
        for slot in range(slots):

            @pl.when(slot < count[section])
            def _():
                row = pl.multiple_of(rows[section, slot] * TILE, TILE)
                col = pl.multiple_of(section * span + cols[section, slot] * TILE, TILE)
                out[pl.ds(row, TILE), pl.ds(col, TILE)] = tiles[section, slot]


def dense_blocks(tiles, rows, cols, count, rows_blk):
    sections = tiles.shape[0]
    shape = (rows_blk, sections * rows_blk)
    return pl.pallas_call(
        dense_kernel,
        out_shape=shape_of(shape),
        in_specs=[SMEM, SMEM, SMEM, VMEM],
        out_specs=VMEM,
        compiler_params=params(),
        cost_estimate=cost(0, tiles.size * 2 + math.prod(shape) * 2),
        name="dense_blocks",
    )(rows, cols, count, tiles)


def window_kernel(pos, planes, out):
    ranks = planes.shape[0]
    place = [pos[2]]
    for step in range(ranks):
        place.append(wrap(place[-1] + 1, ranks))
    for target in range(out.shape[0]):
        section, step = target // ranks, target % ranks
        out[target] = planes[jnp.where(section > pos[1], place[step + 1], place[step])]


def window_pieces(pos, planes, sections):
    ranks = planes.shape[0]
    shape = (sections * ranks,) + planes.shape[1:]
    return pl.pallas_call(
        window_kernel,
        out_shape=shape_of(shape),
        in_specs=[SMEM, VMEM],
        out_specs=VMEM,
        compiler_params=params(),
        cost_estimate=cost(0, math.prod(shape) * 2),
        name="window_pieces",
    )(pos, planes)


def block_order(pos, sections, own, section):
    core = pos[3] if own else 1 - pos[3]
    return wrap(pos[1] + core * (sections // 2) + section, sections)


def forward_kernel(pos, mine, other, blocks, out):
    sections = blocks.shape[0]
    total = None
    for is_own, matrix in ((True, mine), (False, other)):
        side = jnp.concatenate(
            [blocks[block_order(pos, sections, is_own, i)] for i in range(sections // 2)], axis=0
        )
        product = jnp.dot(matrix[...], side, preferred_element_type=F32)
        total = product if total is None else total + product
    out[...] = total.astype(BF16)


def forward_part(pos, mine, other, blocks):
    rows, columns = mine.shape
    width = blocks.shape[-1]
    return pl.pallas_call(
        forward_kernel,
        out_shape=shape_of((rows, width)),
        in_specs=[SMEM, VMEM, VMEM, VMEM],
        out_specs=VMEM,
        compiler_params=params(),
        cost_estimate=cost(4 * rows * columns * width, 4 * rows * columns + blocks.size * 2),
        name="forward_part",
    )(pos, mine, other, blocks)


def layer_kernel(parts, cot, weight, act, out):
    replicas, own, width = parts.shape
    ranks = replicas // 2
    sides = []
    for core in (0, 1):
        side = parts[core].astype(F32)
        for rank in range(1, ranks):
            side += parts[2 * rank + core].astype(F32)
        sides.append(side)
    agg = jnp.concatenate(sides, axis=1).astype(BF16)
    z_value = jnp.dot(agg, weight[...], preferred_element_type=F32)
    sigma = jax.nn.sigmoid(z_value)
    act[...] = (z_value * sigma).astype(BF16)
    slope = cot[...].astype(F32) * sigma * (1.0 + z_value * (1.0 - sigma))
    dz_value = slope.astype(BF16)
    dy_value = lax.dot_general(
        dz_value, weight[...], (((1,), (1,)), ((), ())), preferred_element_type=F32
    ).astype(BF16)
    term = lax.dot_general(
        agg, dz_value, (((0,), (0,)), ((), ())), preferred_element_type=F32
    ).astype(BF16)
    chunk = width // ranks
    for rank in range(ranks):
        for core in (0, 1):
            target = 2 * rank + core
            row = core * width + rank * chunk
            out[target, :own, :] = dy_value[:, core * width : (core + 1) * width]
            out[target, own : own + chunk, :] = term[row : row + chunk, :width]
            out[target, own + chunk :, :] = term[row : row + chunk, width:]


def layer_part(parts, cot, weight):
    replicas, own, width = parts.shape
    out = (replicas, own + 4 * width // replicas, width)
    return pl.pallas_call(
        layer_kernel,
        out_shape=(shape_of(cot.shape), shape_of(out)),
        in_specs=[VMEM] * 3,
        out_specs=(VMEM, VMEM),
        compiler_params=params(),
        cost_estimate=cost(6 * own * 4 * width * width, math.prod(out) * 4),
        name="layer_part",
    )(parts, cot, weight)


def backward_kernel(own, pos, parts, mine, other, out):
    replicas, _, width = parts.shape
    ranks = replicas // 2
    rows = replicas * own
    share = rows // ranks
    piece = parts[0, own:, :].astype(F32)
    for source in range(1, replicas):
        piece += parts[source, own:, :].astype(F32)
    piece = piece.astype(BF16)
    height = out.shape[0] // ranks
    for target in range(ranks):
        out[target * height + rows : (target + 1) * height, :] = piece
    chunks = []
    for rank in range(ranks):
        place = 2 * wrap(pos[0] + rank, ranks)
        chunks += [parts[place, :own, :], parts[place + 1, :own, :]]
    dy_turned = jnp.concatenate(chunks, axis=0).T
    by_block = jnp.where(pos[3] == 0, height, share)
    by_rank = jnp.where(pos[3] == 0, share, height)
    for is_own, matrix in ((True, mine), (False, other)):
        for section in range(ranks // 2):
            side = matrix[:, section * rows : (section + 1) * rows]
            grads = jnp.dot(dy_turned, side, preferred_element_type=F32).astype(BF16).T
            first = block_order(pos, ranks, is_own, section) * by_block
            for rank in range(ranks):
                start = pl.multiple_of(first + rank * by_rank, 16)
                out[pl.ds(start, share), :] = grads[rank * share : (rank + 1) * share, :]


def backward_part(pos, parts, mine, other, own):
    replicas, height, width = parts.shape
    rows, columns = mine.shape
    out = (replicas // 2 * (rows + height - own), width)

    def kernel(*refs):
        backward_kernel(own, *refs)

    return pl.pallas_call(
        kernel,
        out_shape=shape_of(out),
        in_specs=[SMEM, VMEM, VMEM, VMEM],
        out_specs=VMEM,
        compiler_params=params(),
        cost_estimate=cost(4 * rows * columns * width, 4 * rows * columns + math.prod(out) * 2),
        name="backward_part",
    )(pos, parts, mine, other)


def merge_kernel(rows, pos, parts, out):
    ranks, height, width = parts.shape
    share = rows // ranks
    term = parts[0, rows:, :].astype(F32)
    for source in range(1, ranks):
        term += parts[source, rows:, :].astype(F32)
    term = term.astype(BF16)
    for target in range(ranks):
        near = jnp.zeros((share, width), F32)
        far = near
        for source in range(ranks):
            value = parts[source, target * share : (target + 1) * share, :].astype(F32)
            same = (source <= pos[1]) | (pos[3] == 1)
            near += jnp.where(same, value, 0.0)
            far += jnp.where(same, 0.0, value)
        out[target, :share, :] = near.astype(BF16)
        out[target, share : 2 * share, :] = far.astype(BF16)
        out[target, 2 * share :, :] = term


def merge_part(pos, parts, rows):
    ranks, height, width = parts.shape
    shape = (ranks, 2 * rows // ranks + height - rows, width)

    def kernel(*refs):
        merge_kernel(rows, *refs)

    return pl.pallas_call(
        kernel,
        out_shape=shape_of(shape),
        in_specs=[SMEM, VMEM],
        out_specs=VMEM,
        compiler_params=params(),
        cost_estimate=cost(parts.size * 2, parts.size * 2 + math.prod(shape) * 2),
        name="merge_part",
    )(pos, parts)


def place_kernel(share, pos, parts, out):
    ranks, height, width = parts.shape
    own = share // 2
    near = jnp.zeros((share, width), F32)
    far = near
    term = jnp.zeros((height - 2 * share, width), F32)
    for source in range(ranks):
        first = parts[source, :share, :].astype(F32)
        second = parts[source, share : 2 * share, :].astype(F32)
        same = (source <= pos[1]) | (pos[3] == 0)
        near += jnp.where(same, first, 0.0)
        far += jnp.where(same, second, first)
        term += parts[source, 2 * share :, :].astype(F32)
    near, far, term = near.astype(BF16), far.astype(BF16), term.astype(BF16)
    plane = wrap(pos[0] + pos[2], ranks)
    behind = wrap(plane + 1, ranks)
    nothing = jnp.zeros_like(near)
    for target in range(ranks):
        value = jnp.where(plane == target, near, jnp.where(behind == target, far, nothing))
        for core in (0, 1):
            out[2 * target + core, :own, :] = value[core * own : (core + 1) * own, :]
            out[2 * target + core, own:, :] = term


def place_part(pos, parts, share):
    ranks, height, width = parts.shape
    shape = (2 * ranks, height - 3 * share // 2, width)

    def kernel(*refs):
        place_kernel(share, *refs)

    return pl.pallas_call(
        kernel,
        out_shape=shape_of(shape),
        in_specs=[SMEM, VMEM],
        out_specs=VMEM,
        compiler_params=params(),
        cost_estimate=cost(parts.size, parts.size * 2 + math.prod(shape) * 2),
        name="place_part",
    )(pos, parts)


def finish_kernel(scale, pos, parts, term, grads):
    replicas, height, width = parts.shape
    ranks = replicas // 2
    own = grads.shape[0]
    chunk = width // ranks
    for core in (0, 1):
        total = parts[core, :own, :].astype(F32)
        for depth in range(1, ranks):
            total += parts[2 * depth + core, :own, :].astype(F32)
        grads[:, core * width : (core + 1) * width] = total.astype(BF16)
        for depth in range(ranks):
            row = core * width + wrap(pos[2] + depth, ranks) * chunk
            for side in (0, 1):
                first = own + side * chunk
                value = parts[2 * depth + core, first : first + chunk, :].astype(F32) / scale
                term[pl.ds(pl.multiple_of(row, chunk), chunk), side * width : (side + 1) * width] = value


def finish_part(pos, parts, own, nodes):
    width = parts.shape[2]

    def kernel(*refs):
        finish_kernel(math.sqrt(nodes), *refs)

    return pl.pallas_call(
        kernel,
        out_shape=(shape_of((2 * width, 2 * width), F32), shape_of((own, 2 * width))),
        in_specs=[SMEM, VMEM],
        out_specs=(VMEM, VMEM),
        compiler_params=params(),
        cost_estimate=cost(parts.size, parts.size * 2),
        name="finish_part",
    )(pos, parts)


def device_at(ranks, depth, section, rank, core):
    return ((depth % ranks * ranks + section) * ranks + rank) * 2 + core


def section_groups(ranks):
    every = [(a, b) for a in range(ranks) for b in range(ranks)]
    steps = range(ranks)
    line = [[device_at(ranks, a, k, b, 0) for k in steps] for a, b in every]
    slant = [[device_at(ranks, a - k, b, k, 1) for k in steps] for a, b in every]
    return line + slant


def share_groups(ranks):
    return [[device ^ 1 for device in group] for group in section_groups(ranks)]


def plane_groups(ranks):
    return [
        [device_at(ranks, i - rank, section, rank, core) for i in range(ranks)]
        for section in range(ranks)
        for rank in range(ranks)
        for core in (0, 1)
    ]


def window_groups(ranks):
    return [
        [
            device_at(ranks, depth, section, (i - depth) % ranks, core)
            for section in range(ranks)
            for i in range(ranks)
        ]
        for depth in range(ranks)
        for core in (0, 1)
    ]


def replica_groups(ranks):
    return [
        [
            device_at(ranks, depth, section, (i - depth) % ranks, core)
            for i in range(ranks)
            for core in (0, 1)
        ]
        for depth in range(ranks)
        for section in range(ranks)
    ]


def grouped(pieces, lists):
    return lax.all_to_all(
        pieces,
        ("z", "y", "x", "core"),
        split_axis=0,
        concat_axis=0,
        axis_index_groups=lists,
        tiled=True,
    )


def exchange(pieces, axis):
    return lax.all_to_all(pieces, axis, split_axis=0, concat_axis=0, tiled=True)


def per_device(features, weight, cotangent, tile_values, tile_rows, tile_cols, tile_count):
    rows, columns = features.shape
    width = columns // 2
    ranks = lax.axis_size("x")
    share = rows // ranks
    own = share // 2
    pos = jnp.stack([lax.axis_index(name) for name in ("z", "y", "x", "core")]).astype(jnp.int32)

    half = lax.dynamic_slice_in_dim(features, lax.axis_index("core") * width, width, axis=1)
    half, tile_rows, tile_cols, tile_count = lax.optimization_barrier(
        (half, tile_rows, tile_cols, tile_count)
    )
    planes = grouped(half.reshape(ranks, share, width), plane_groups(ranks))
    mine = dense_blocks(tile_values[0], tile_rows[0], tile_cols[0], tile_count[0], rows)
    pieces, mine = lax.optimization_barrier((window_pieces(pos, planes, ranks), mine))
    other = lax.ppermute(mine, "core", [(0, 1), (1, 0)])
    blocks = grouped(pieces, window_groups(ranks))
    part = forward_part(pos, mine, other, blocks.reshape(ranks, rows, width))
    parts = exchange(part.reshape(2 * ranks, own, width), ("x", "core"))
    activations, pieces = layer_part(parts, cotangent, weight)
    parts = grouped(pieces, replica_groups(ranks))
    pieces = backward_part(pos, parts, mine, other, own)
    parts = grouped(pieces, section_groups(ranks)).reshape(ranks, -1, width)
    parts = grouped(merge_part(pos, parts, rows), share_groups(ranks))
    parts = exchange(place_part(pos, parts, share), ("z", "core"))
    weight_grad, feature_grad = finish_part(pos, parts, own, rows * ranks * ranks)
    return (activations, weight_grad, feature_grad)


def solution(mesh):
    blk, rep = mesh.devices.shape
    ranks = rep // 2
    devices = mesh.devices.reshape(ranks, blk // ranks, ranks, 2)
    grid = Mesh(devices, ("z", "y", "x", "core"))
    blk_axes, rep_axes = ("z", "y"), ("x", "core")
    return jax.shard_map(
        per_device,
        mesh=grid,
        in_specs=(
            P(blk_axes, None),
            P(),
            P(blk_axes + rep_axes, None),
            P(blk_axes, rep_axes, None, None, None),
            P(blk_axes, rep_axes, None),
            P(blk_axes, rep_axes, None),
            P(blk_axes, rep_axes),
        ),
        out_specs=(P(blk_axes + rep_axes, None), P(), P(blk_axes + rep_axes, None)),
        check_vma=False,
    )
```

```python
import math

import jax
import jax.numpy as jnp
from jax import lax
from jax.experimental import pallas as pl
from jax.experimental.pallas import tpu as pltpu
from jax.sharding import Mesh
from jax.sharding import PartitionSpec as P

TILE = 128
BF16 = jnp.bfloat16
F32 = jnp.float32
VMEM = pl.BlockSpec(memory_space=pltpu.VMEM)
SMEM = pl.BlockSpec(memory_space=pltpu.SMEM)


def params(mib=40):
    return pltpu.CompilerParams(vmem_limit_bytes=mib << 20)


def shape_of(shape, dtype=BF16):
    return jax.ShapeDtypeStruct(shape, dtype)


def cost(flops, nbytes):
    return pl.CostEstimate(flops=flops, bytes_accessed=nbytes, transcendentals=0)


def wrap(index, size):
    return jnp.where(index >= size, index - size, index)


def dense_kernel(rows, cols, count, tiles, out):
    sections, slots = tiles.shape[:2]
    span = out.shape[0]
    for section in range(sections):
        out[:, section * span : (section + 1) * span] = jnp.zeros((span, span), BF16)
        for slot in range(slots):

            @pl.when(slot < count[section])
            def _():
                row = pl.multiple_of(rows[section, slot] * TILE, TILE)
                col = pl.multiple_of(section * span + cols[section, slot] * TILE, TILE)
                out[pl.ds(row, TILE), pl.ds(col, TILE)] = tiles[section, slot]


def dense_blocks(tiles, rows, cols, count, rows_blk):
    sections = tiles.shape[0]
    shape = (rows_blk, sections * rows_blk)
    return pl.pallas_call(
        dense_kernel,
        out_shape=shape_of(shape),
        in_specs=[SMEM, SMEM, SMEM, VMEM],
        out_specs=VMEM,
        compiler_params=params(),
        cost_estimate=cost(0, tiles.size * 2 + math.prod(shape) * 2),
        name="dense_blocks",
    )(rows, cols, count, tiles)


def light_kernel(pos, planes, out):
    ranks, share = planes.shape[:2]
    second_core = pos[3] == 1
    here = wrap(pos[0] + pos[2], ranks)
    place = [pos[2]]
    for step in range(ranks):
        place.append(wrap(place[-1] + 1, ranks))
    for target in range(ranks):
        ahead = wrap(here + (target > pos[1]).astype(jnp.int32), ranks)
        out[target, :share, :] = planes[jnp.where(second_core, ahead, place[target])]
        out[target, share:, :] = planes[place[target + 1]]


def light_pieces(pos, planes):
    ranks, share, width = planes.shape
    shape = (ranks, 2 * share, width)
    return pl.pallas_call(
        light_kernel,
        out_shape=shape_of(shape),
        in_specs=[SMEM, VMEM],
        out_specs=VMEM,
        compiler_params=params(),
        cost_estimate=cost(0, math.prod(shape) * 2),
        name="light_pieces",
    )(pos, planes)


def heavy_kernel(pos, parts, out):
    ranks, height, width = parts.shape
    share = height // 2
    near = parts[:, :share, :].reshape(ranks * share, width)
    for target in range(ranks):
        out[target] = near

    @pl.when(pos[3] == 0)
    def _():
        far = parts[:, share:, :].reshape(ranks * share, width)
        for target in range(ranks):

            @pl.when(target > pos[1])
            def _():
                out[target] = far


def heavy_pieces(pos, parts):
    ranks, height, width = parts.shape
    shape = (ranks, ranks * height // 2, width)
    return pl.pallas_call(
        heavy_kernel,
        out_shape=shape_of(shape),
        in_specs=[SMEM, VMEM],
        out_specs=VMEM,
        compiler_params=params(),
        cost_estimate=cost(0, math.prod(shape) * 2),
        name="heavy_pieces",
    )(pos, parts)


def block_order(pos, sections, own, section):
    core = pos[3] if own else 1 - pos[3]
    return wrap(pos[1] + core * (sections // 2) + section, sections)


def forward_kernel(pos, mine, other, blocks, out):
    rows, width = out.shape
    sections = blocks.shape[0] // rows
    share = rows // sections
    by_block = jnp.where(pos[3] == 0, rows, share)
    by_slice = jnp.where(pos[3] == 0, share, rows)
    total = None
    for is_own, matrix in ((True, mine), (False, other)):
        slices = []
        for section in range(sections // 2):
            first = block_order(pos, sections, is_own, section) * by_block
            for i in range(sections):
                start = pl.multiple_of(first + i * by_slice, 16)
                slices.append(blocks[pl.ds(start, share), :])
        side = jnp.concatenate(slices, axis=0)
        product = jnp.dot(matrix[...], side, preferred_element_type=F32)
        total = product if total is None else total + product
    out[...] = total.astype(BF16)


def forward_part(pos, mine, other, blocks):
    rows, columns = mine.shape
    width = blocks.shape[-1]
    return pl.pallas_call(
        forward_kernel,
        out_shape=shape_of((rows, width)),
        in_specs=[SMEM, VMEM, VMEM, VMEM],
        out_specs=VMEM,
        compiler_params=params(),
        cost_estimate=cost(4 * rows * columns * width, 4 * rows * columns + blocks.size * 2),
        name="forward_part",
    )(pos, mine, other, blocks)


def layer_kernel(parts, cot, weight, act, out):
    replicas, own, width = parts.shape
    ranks = replicas // 2
    sides = []
    for core in (0, 1):
        side = parts[core].astype(F32)
        for rank in range(1, ranks):
            side += parts[2 * rank + core].astype(F32)
        sides.append(side)
    agg = jnp.concatenate(sides, axis=1).astype(BF16)
    z_value = jnp.dot(agg, weight[...], preferred_element_type=F32)
    sigma = jax.nn.sigmoid(z_value)
    act[...] = (z_value * sigma).astype(BF16)
    slope = cot[...].astype(F32) * sigma * (1.0 + z_value * (1.0 - sigma))
    dz_value = slope.astype(BF16)
    dy_value = lax.dot_general(
        dz_value, weight[...], (((1,), (1,)), ((), ())), preferred_element_type=F32
    ).astype(BF16)
    term = lax.dot_general(
        agg, dz_value, (((0,), (0,)), ((), ())), preferred_element_type=F32
    ).astype(BF16)
    chunk = width // ranks
    for rank in range(ranks):
        for core in (0, 1):
            target = 2 * rank + core
            row = core * width + rank * chunk
            out[target, :own, :] = dy_value[:, core * width : (core + 1) * width]
            out[target, own : own + chunk, :] = term[row : row + chunk, :width]
            out[target, own + chunk :, :] = term[row : row + chunk, width:]


def layer_part(parts, cot, weight):
    replicas, own, width = parts.shape
    out = (replicas, own + 4 * width // replicas, width)
    return pl.pallas_call(
        layer_kernel,
        out_shape=(shape_of(cot.shape), shape_of(out)),
        in_specs=[VMEM] * 3,
        out_specs=(VMEM, VMEM),
        compiler_params=params(),
        cost_estimate=cost(6 * own * 4 * width * width, math.prod(out) * 4),
        name="layer_part",
    )(parts, cot, weight)


def backward_kernel(own, pos, parts, mine, other, out):
    replicas, _, width = parts.shape
    ranks = replicas // 2
    rows = replicas * own
    share = rows // ranks
    piece = parts[0, own:, :].astype(F32)
    for source in range(1, replicas):
        piece += parts[source, own:, :].astype(F32)
    piece = piece.astype(BF16)
    height = out.shape[0] // ranks
    for target in range(ranks):
        out[target * height + rows : (target + 1) * height, :] = piece
    chunks = []
    for rank in range(ranks):
        place = 2 * wrap(pos[0] + rank, ranks)
        chunks += [parts[place, :own, :], parts[place + 1, :own, :]]
    dy_turned = jnp.concatenate(chunks, axis=0).T
    by_block = jnp.where(pos[3] == 0, height, share)
    by_rank = jnp.where(pos[3] == 0, share, height)
    for is_own, matrix in ((True, mine), (False, other)):
        for section in range(ranks // 2):
            side = matrix[:, section * rows : (section + 1) * rows]
            grads = jnp.dot(dy_turned, side, preferred_element_type=F32).astype(BF16).T
            first = block_order(pos, ranks, is_own, section) * by_block
            for rank in range(ranks):
                start = pl.multiple_of(first + rank * by_rank, 16)
                out[pl.ds(start, share), :] = grads[rank * share : (rank + 1) * share, :]


def backward_part(pos, parts, mine, other, own):
    replicas, height, width = parts.shape
    rows, columns = mine.shape
    out = (replicas // 2 * (rows + height - own), width)

    def kernel(*refs):
        backward_kernel(own, *refs)

    return pl.pallas_call(
        kernel,
        out_shape=shape_of(out),
        in_specs=[SMEM, VMEM, VMEM, VMEM],
        out_specs=VMEM,
        compiler_params=params(),
        cost_estimate=cost(4 * rows * columns * width, 4 * rows * columns + math.prod(out) * 2),
        name="backward_part",
    )(pos, parts, mine, other)


def merge_kernel(rows, pos, parts, out):
    ranks, height, width = parts.shape
    share = rows // ranks
    term = parts[0, rows:, :].astype(F32)
    for source in range(1, ranks):
        term += parts[source, rows:, :].astype(F32)
    term = term.astype(BF16)
    for target in range(ranks):
        near = jnp.zeros((share, width), F32)
        far = near
        for source in range(ranks):
            value = parts[source, target * share : (target + 1) * share, :].astype(F32)
            same = (source <= pos[1]) | (pos[3] == 1)
            near += jnp.where(same, value, 0.0)
            far += jnp.where(same, 0.0, value)
        out[target, :share, :] = near.astype(BF16)
        out[target, share : 2 * share, :] = far.astype(BF16)
        out[target, 2 * share :, :] = term


def merge_part(pos, parts, rows):
    ranks, height, width = parts.shape
    shape = (ranks, 2 * rows // ranks + height - rows, width)

    def kernel(*refs):
        merge_kernel(rows, *refs)

    return pl.pallas_call(
        kernel,
        out_shape=shape_of(shape),
        in_specs=[SMEM, VMEM],
        out_specs=VMEM,
        compiler_params=params(),
        cost_estimate=cost(parts.size * 2, parts.size * 2 + math.prod(shape) * 2),
        name="merge_part",
    )(pos, parts)


def place_kernel(share, pos, parts, out):
    ranks, height, width = parts.shape
    own = share // 2
    near = jnp.zeros((share, width), F32)
    far = near
    term = jnp.zeros((height - 2 * share, width), F32)
    for source in range(ranks):
        first = parts[source, :share, :].astype(F32)
        second = parts[source, share : 2 * share, :].astype(F32)
        same = (source <= pos[1]) | (pos[3] == 0)
        near += jnp.where(same, first, 0.0)
        far += jnp.where(same, second, first)
        term += parts[source, 2 * share :, :].astype(F32)
    near, far, term = near.astype(BF16), far.astype(BF16), term.astype(BF16)
    plane = wrap(pos[0] + pos[2], ranks)
    behind = wrap(plane + 1, ranks)
    nothing = jnp.zeros_like(near)
    for target in range(ranks):
        value = jnp.where(plane == target, near, jnp.where(behind == target, far, nothing))
        for core in (0, 1):
            out[2 * target + core, :own, :] = value[core * own : (core + 1) * own, :]
            out[2 * target + core, own:, :] = term


def place_part(pos, parts, share):
    ranks, height, width = parts.shape
    shape = (2 * ranks, height - 3 * share // 2, width)

    def kernel(*refs):
        place_kernel(share, *refs)

    return pl.pallas_call(
        kernel,
        out_shape=shape_of(shape),
        in_specs=[SMEM, VMEM],
        out_specs=VMEM,
        compiler_params=params(),
        cost_estimate=cost(parts.size, parts.size * 2 + math.prod(shape) * 2),
        name="place_part",
    )(pos, parts)


def finish_kernel(scale, pos, parts, term, grads):
    replicas, height, width = parts.shape
    ranks = replicas // 2
    own = grads.shape[0]
    chunk = width // ranks
    for core in (0, 1):
        total = parts[core, :own, :].astype(F32)
        for depth in range(1, ranks):
            total += parts[2 * depth + core, :own, :].astype(F32)
        grads[:, core * width : (core + 1) * width] = total.astype(BF16)
        for depth in range(ranks):
            row = core * width + wrap(pos[2] + depth, ranks) * chunk
            for side in (0, 1):
                first = own + side * chunk
                value = parts[2 * depth + core, first : first + chunk, :].astype(F32) / scale
                term[pl.ds(pl.multiple_of(row, chunk), chunk), side * width : (side + 1) * width] = value


def finish_part(pos, parts, own, nodes):
    width = parts.shape[2]

    def kernel(*refs):
        finish_kernel(math.sqrt(nodes), *refs)

    return pl.pallas_call(
        kernel,
        out_shape=(shape_of((2 * width, 2 * width), F32), shape_of((own, 2 * width))),
        in_specs=[SMEM, VMEM],
        out_specs=(VMEM, VMEM),
        compiler_params=params(),
        cost_estimate=cost(parts.size, parts.size * 2),
        name="finish_part",
    )(pos, parts)


def device_at(ranks, depth, section, rank, core):
    return ((depth % ranks * ranks + section) * ranks + rank) * 2 + core


def section_groups(ranks):
    every = [(a, b) for a in range(ranks) for b in range(ranks)]
    steps = range(ranks)
    line = [[device_at(ranks, a, k, b, 0) for k in steps] for a, b in every]
    slant = [[device_at(ranks, a - k, b, k, 1) for k in steps] for a, b in every]
    return line + slant


def share_groups(ranks):
    return [[device ^ 1 for device in group] for group in section_groups(ranks)]


def plane_groups(ranks):
    return [
        [device_at(ranks, i - rank * (1 - core), section, rank, core) for i in range(ranks)]
        for section in range(ranks)
        for rank in range(ranks)
        for core in (0, 1)
    ]


def light_groups(ranks):
    every = [(a, b) for a in range(ranks) for b in range(ranks)]
    steps = range(ranks)
    row = [[device_at(ranks, a, b, (i - a) % ranks, 0) for i in steps] for a, b in every]
    line = [[device_at(ranks, a, k, b, 1) for k in steps] for a, b in every]
    return row + line


def heavy_groups(ranks):
    every = [(a, b) for a in range(ranks) for b in range(ranks)]
    steps = range(ranks)
    line = [[device_at(ranks, a, k, b, 0) for k in steps] for a, b in every]
    slant = [[device_at(ranks, i, b, (a - i) % ranks, 1) for i in steps] for a, b in every]
    return line + slant


def replica_groups(ranks):
    return [
        [
            device_at(ranks, depth, section, (i - depth) % ranks, core)
            for i in range(ranks)
            for core in (0, 1)
        ]
        for depth in range(ranks)
        for section in range(ranks)
    ]


def grouped(pieces, lists):
    return lax.all_to_all(
        pieces,
        ("z", "y", "x", "core"),
        split_axis=0,
        concat_axis=0,
        axis_index_groups=lists,
        tiled=True,
    )


def exchange(pieces, axis):
    return lax.all_to_all(pieces, axis, split_axis=0, concat_axis=0, tiled=True)


def per_device(features, weight, cotangent, tile_values, tile_rows, tile_cols, tile_count):
    rows, columns = features.shape
    width = columns // 2
    ranks = lax.axis_size("x")
    share = rows // ranks
    own = share // 2
    pos = jnp.stack([lax.axis_index(name) for name in ("z", "y", "x", "core")]).astype(jnp.int32)

    half = lax.dynamic_slice_in_dim(features, lax.axis_index("core") * width, width, axis=1)
    half, tile_rows, tile_cols, tile_count = lax.optimization_barrier(
        (half, tile_rows, tile_cols, tile_count)
    )
    planes = grouped(half.reshape(ranks, share, width), plane_groups(ranks))
    mine = dense_blocks(tile_values[0], tile_rows[0], tile_cols[0], tile_count[0], rows)
    pieces, mine = lax.optimization_barrier((light_pieces(pos, planes), mine))
    other = lax.ppermute(mine, "core", [(0, 1), (1, 0)])
    parts = grouped(pieces, light_groups(ranks))
    pieces, other = lax.optimization_barrier((heavy_pieces(pos, parts), other))
    blocks = grouped(pieces, heavy_groups(ranks))
    part = forward_part(pos, mine, other, blocks.reshape(ranks * rows, width))
    parts = exchange(part.reshape(2 * ranks, own, width), ("x", "core"))
    activations, pieces = layer_part(parts, cotangent, weight)
    parts = grouped(pieces, replica_groups(ranks))
    pieces = backward_part(pos, parts, mine, other, own)
    parts = grouped(pieces, section_groups(ranks)).reshape(ranks, -1, width)
    parts = grouped(merge_part(pos, parts, rows), share_groups(ranks))
    parts = exchange(place_part(pos, parts, share), ("z", "core"))
    weight_grad, feature_grad = finish_part(pos, parts, own, rows * ranks * ranks)
    return (activations, weight_grad, feature_grad)


def solution(mesh):
    blk, rep = mesh.devices.shape
    ranks = rep // 2
    devices = mesh.devices.reshape(ranks, blk // ranks, ranks, 2)
    grid = Mesh(devices, ("z", "y", "x", "core"))
    blk_axes, rep_axes = ("z", "y"), ("x", "core")
    return jax.shard_map(
        per_device,
        mesh=grid,
        in_specs=(
            P(blk_axes, None),
            P(),
            P(blk_axes + rep_axes, None),
            P(blk_axes, rep_axes, None, None, None),
            P(blk_axes, rep_axes, None),
            P(blk_axes, rep_axes, None),
            P(blk_axes, rep_axes),
        ),
        out_specs=(P(blk_axes + rep_axes, None), P(), P(blk_axes + rep_axes, None)),
        check_vma=False,
    )
```
